32 devices in a mesh: dom: 8 (over z, y), rep: 4 (over x, core).
Axes of the slice: x: 2, y: 2, z: 4, core: 2. Of those that a mesh axis runs over, the one named last changes fastest.
Arguments:
- feats: bfloat16 [8192, 256], P('dom'), may hold values from -6 to 6
- history: bfloat16 [8192, 256], P('dom'), may hold values from -6 to 6
- adj_inner: bfloat16 [8192, 1024], P('dom'), may hold values from -0.15625 to 0.15625
- adj_halo: bfloat16 [8192, 256], P('dom'), may hold values from -0.15625 to 0.15625
- halo_rows: int32 [64, 32], P('dom'), may hold values from 0 to 1023
- w_self: bfloat16 [256, 256], replicated, may hold values from -0.375 to 0.375
- w_nbr: bfloat16 [256, 256], replicated, may hold values from -0.375 to 0.375
- b_enc: float32 [256], replicated, may hold values from -3 to 3
- edge_owner: int32 [8192, 2], P(('dom', 'rep')), may hold values from 0 to 7, all different within a row; in each aligned block of 256 rows (0 to 255, 256 to 511, ...) at most 128 rows name the same one
- edge_rows: int32 [8192, 2], P(('dom', 'rep')), may hold values from 0 to 1023
- labels: int32 [8192], P(('dom', 'rep')), may hold values 0 or 1
- w_dec1: bfloat16 [256, 256], replicated, may hold values from -0.375 to 0.375
- b_dec1: float32 [256], replicated, may hold values from -3 to 3
- w_dec2: bfloat16 [256], replicated, may hold values from -0.375 to 0.375
Outputs:
- embed: bfloat16 [8192, 256], P('dom')
- grad_embed: float32 [8192, 256], P(('dom', 'rep'))
- grad_dec1: float32 [256, 256], replicated
- grad_bias1: float32 [256], replicated
- grad_dec2: float32 [256], replicated
The draws below stay inside these ranges and needn't reach their ends.
Inputs may be any that keep to these rules, and one draw needn't show every extreme that they name: `edge_owner`: among the rows of one device, no owner is named by more than 128 endpoints, a bound that some block reaches; the two endpoints of an edge have different owners.
All inputs are finite; a program needn't handle non-finite values. No bound on the sum of `labels` on one device may be relied on, other than what follows from the above.
Results may differ from the reference program's by a relative error of at most 0.0069.
Values may be sent and summed in bfloat16 or wider, within the bound.
No kernel may reach another device: no remote copies, remote signals or barrier semaphores. Data moves between devices by JAX's collectives and lax.ppermute only.
A program may use at most 64 MiB of HBM per device.

```python
import math
import jax
import jax.numpy as jnp
import numpy as np
from jax import lax

W = 256
NPD = 1024
HALO = 256
QDEV = 256
NODES = 8192
CAP_H = 32
CAP_E = 128
Q_TOTAL = 8192
N_DOM = 8


def set_ends(result, own_key, low, top_value):
    index_at = [jax.random.randint(jax.random.fold_in(own_key, axis), (), 0, length) for axis, length in enumerate(result.shape)]
    main_axis = result.shape.index(max(result.shape))
    neighbour = index_at[:main_axis] + [(index_at[main_axis] + 1) % result.shape[main_axis]] + index_at[main_axis + 1:]
    return result.at[tuple(index_at)].set(low).at[tuple(neighbour)].set(top_value)


def level_of(rng, extent, cuts, least, top_value):
    def one(dim, blocks):
        heights = jax.random.uniform(jax.random.fold_in(jax.random.fold_in(rng, 6), dim), (blocks,), jnp.float32, least / len(cuts), top_value / len(cuts))
        return jnp.repeat(jnp.exp(heights), extent[dim] // blocks).reshape((-1,) + (1,) * (len(extent) - dim - 1))

    level = one(*cuts[0])
    for cut in cuts[1:]:
        level = level * one(*cut)
    return level


def shared_out(stream_key, own, number, rows, number_of, top, bound, slope):
    ranking = jax.random.permutation(stream_key, number_of)
    crowded, ordinary = portions_of(number_of, rows * top, bound, slope, True), portions_of(number_of, rows * top, bound, slope, False)
    places = jnp.arange(number_of)

    def named(lengths, turn):
        used = int((lengths > 0).sum())
        fixed = max(1, used // 4)
        passed = fixed + (places - fixed + turn * (used - fixed)) % max(1, number_of - fixed)
        return jnp.zeros((number_of,), jnp.int32).at[ranking[jnp.where(places < fixed, places, passed)]].set(jnp.asarray(lengths, jnp.int32))

    lengths = jnp.where(number % 4 == 0, named(crowded, number // 4), named(ordinary, number - number // 4 - 1))
    mixed = jax.random.permutation(jax.random.fold_in(own, 3), number_of)
    giver, sink = mixed[0:number_of // 2 * 2:2], mixed[1:number_of // 2 * 2:2]
    margin = jnp.minimum(lengths[giver] - 1, bound - lengths[sink]) // 2
    margin = jnp.where((giver == ranking[0]) | (sink == ranking[0]) | (lengths[sink] == 0), 0, jnp.maximum(margin, 0))
    passed = jax.random.randint(jax.random.fold_in(own, 4), (number_of // 2,), 0, 1 << 20) % (margin + 1)
    lengths = lengths.at[giver].add(-passed).at[sink].add(passed)
    items = jnp.searchsorted(jnp.cumsum(lengths), jnp.arange(rows * top), side="right").astype(jnp.int32)
    grid = items.reshape(top, rows).T
    grid = grid[jax.random.permutation(jax.random.fold_in(own, 1), rows)]
    turn = jax.random.randint(jax.random.fold_in(own, 2), (rows, 1), 0, top)
    return jnp.take_along_axis(grid, (jnp.arange(top)[None, :] + turn) % top, axis=1)


def portions_of(number_of, total, most, lean, full):
    weights = [(1 << 20) // math.isqrt(rank ** lean) + 1 for rank in range(1, number_of + 1)]
    largest = most if full else min(most, max(-(-total // number_of), total * weights[0] // sum(weights)))
    least = 1 if total - largest >= number_of - 1 else 0
    counts, rest = [largest] + [least] * (number_of - 1), total - largest - least * (number_of - 1)
    while rest > 0:
        movable = [i for i in range(1, number_of) if counts[i] < largest] or [i for i in range(1, number_of) if counts[i] < most]
        pool, remaining = sum([weights[i] for i in movable]), rest
        for i in movable:
            more = min(most - counts[i], max(1, remaining * weights[i] // pool), rest)
            counts[i] = counts[i] + more
            rest = rest - more
    return np.array(counts)


def scatter_about(rng, extent, spread, reach, pieces=(), held_as=jnp.bfloat16):
    array = jax.random.normal(rng, extent, jnp.float32) * spread
    if len(pieces) > 0:
        array = level_of(rng, extent, pieces, -0.22, 0.18) * array
    return jnp.clip(array, min=-reach, max=reach).astype(held_as)


def setup_inputs(seed: int = 0) -> dict:
    streams_of = jax.random.split(jax.random.key(seed), 15)
    feats = scatter_about(streams_of[0], (NODES, W), 1.0, 6.0, ((0, 8),))
    history = scatter_about(streams_of[1], (NODES, W), 1.0, 6.0, ((0, 8),))
    adj_inner = scatter_about(streams_of[2], (NODES, NPD), (NPD + HALO) ** -0.5, 0.15625, ((0, 8),))
    adj_halo = scatter_about(streams_of[3], (NODES, HALO), (NPD + HALO) ** -0.5, 0.15625, ((0, 8),))
    halo_rows = set_ends(jax.random.randint(streams_of[4], (N_DOM * N_DOM, CAP_H), 0, NPD), jax.random.fold_in(streams_of[4], 1), 0, NPD - 1).astype(jnp.int32)
    w_self = scatter_about(streams_of[5], (W, W), W ** -0.5, 0.375)
    w_nbr = scatter_about(streams_of[6], (W, W), W ** -0.5, 0.375)
    b_enc = scatter_about(streams_of[7], (W,), 0.5, 3.0, (), jnp.float32)
    edge_owner_keys = jax.random.split(jax.random.fold_in(streams_of[8], 1), Q_TOTAL // QDEV)
    edge_owner_turns = jax.random.permutation(jax.random.fold_in(streams_of[8], 3), Q_TOTAL // QDEV)
    edge_owner = jax.vmap(lambda own, number: shared_out(jax.random.fold_in(streams_of[8], 2), own, number, QDEV, N_DOM, 2, CAP_E, 2))(edge_owner_keys, edge_owner_turns).reshape((Q_TOTAL, 2))
    edge_rows = set_ends(jax.random.randint(streams_of[9], (Q_TOTAL, 2), 0, NPD), jax.random.fold_in(streams_of[9], 1), 0, NPD - 1).astype(jnp.int32)
    labels = set_ends((jax.random.randint(streams_of[10], (Q_TOTAL,), 0, 2) < 1).astype(jnp.int32), jax.random.fold_in(streams_of[10], 1), 0, 1)
    w_dec1 = scatter_about(streams_of[11], (W, W), W ** -0.5, 0.375)
    b_dec1 = scatter_about(streams_of[12], (W,), 0.5, 3.0, (), jnp.float32)
    w_dec2 = scatter_about(streams_of[13], (W,), W ** -0.5, 0.375)
    return {"feats": feats, "history": history, "adj_inner": adj_inner, "adj_halo": adj_halo, "halo_rows": halo_rows, "w_self": w_self, "w_nbr": w_nbr, "b_enc": b_enc, "edge_owner": edge_owner, "edge_rows": edge_rows, "labels": labels, "w_dec1": w_dec1, "b_dec1": b_dec1, "w_dec2": w_dec2}


def encode_block(rows_x, a_inner, a_halo, all_x, halo, w_self, w_nbr, b_enc):
    agg = (jnp.dot(a_inner, all_x, preferred_element_type=jnp.float32)
           + jnp.dot(a_halo, halo, preferred_element_type=jnp.float32)).astype(jnp.bfloat16)
    pre = (jnp.dot(rows_x, w_self, preferred_element_type=jnp.float32)
           + jnp.dot(agg, w_nbr, preferred_element_type=jnp.float32) + b_enc)
    return jnp.maximum(pre, 0.0).astype(jnp.bfloat16)


def decode(head, tail, target, w_dec1, b_dec1, w_dec2):
    zprod = (head.astype(jnp.float32) * tail.astype(jnp.float32)).astype(jnp.bfloat16)
    pre = jnp.dot(zprod, w_dec1, preferred_element_type=jnp.float32) + b_dec1
    sig = jax.nn.sigmoid(pre)
    hidden = (pre * sig).astype(jnp.bfloat16)
    logit = jnp.dot(hidden, w_dec2, preferred_element_type=jnp.float32)
    dlogit = jax.nn.sigmoid(logit) - target
    d_pre = (dlogit[:, None] * w_dec2.astype(jnp.float32) * (sig * (1.0 + pre * (1.0 - sig)))).astype(jnp.bfloat16)
    grad_w1 = jnp.dot(zprod.T, d_pre, preferred_element_type=jnp.float32)
    grad_b1 = jnp.sum(d_pre.astype(jnp.float32), axis=0)
    grad_w2 = jnp.sum(hidden.astype(jnp.float32) * dlogit[:, None], axis=0)
    dzval = jnp.dot(d_pre, w_dec1.T, preferred_element_type=jnp.float32)
    return dzval * tail.astype(jnp.float32), dzval * head.astype(jnp.float32), grad_w1, grad_b1, grad_w2


def reference(feats, history, adj_inner, adj_halo, halo_rows, w_self, w_nbr, b_enc,
              edge_owner, edge_rows, labels, w_dec1, b_dec1, w_dec2):
    def one_cluster(part):
        start = part * NPD
        rows_x = lax.dynamic_slice_in_dim(feats, start, NPD, 0)
        a_inner = lax.dynamic_slice_in_dim(adj_inner, start, NPD, 0)
        a_halo = lax.dynamic_slice_in_dim(adj_halo, start, NPD, 0)
        wanted = lax.dynamic_slice_in_dim(halo_rows, part * N_DOM, N_DOM, 0)
        owners = jnp.arange(N_DOM, dtype=jnp.int32)[:, None] * NPD
        glob = (owners + wanted).reshape(-1).astype(jnp.int32)
        halo = history[glob]
        return encode_block(rows_x, a_inner, a_halo, rows_x, halo, w_self, w_nbr, b_enc)

    embed = lax.map(one_cluster, jnp.arange(N_DOM, dtype=jnp.int32)).reshape(NODES, W)

    def step(carry, block):
        gacc, acc1, accb, acc2 = carry
        start = block * QDEV
        owner = lax.dynamic_slice_in_dim(edge_owner, start, QDEV, 0)
        local = lax.dynamic_slice_in_dim(edge_rows, start, QDEV, 0)
        target = lax.dynamic_slice_in_dim(labels, start, QDEV, 0).astype(jnp.float32)
        index = (owner * NPD + local).astype(jnp.int32)
        head = embed[index[:, 0]]
        tail = embed[index[:, 1]]
        g_head, g_tail, gw1, gb1, gw2 = decode(head, tail, target, w_dec1, b_dec1, w_dec2)
        gacc = gacc.at[index[:, 0]].add(g_head).at[index[:, 1]].add(g_tail)
        return (gacc, acc1 + gw1, accb + gb1, acc2 + gw2), None

    init = (jnp.zeros((NODES, W), jnp.float32), jnp.zeros((W, W), jnp.float32),
            jnp.zeros((W,), jnp.float32), jnp.zeros((W,), jnp.float32))
    blocks = jnp.arange(Q_TOTAL // QDEV, dtype=jnp.int32)
    (grad_embed, grad_dec1, grad_bias1, grad_dec2), _ = lax.scan(step, init, blocks)
    return embed, grad_embed, grad_dec1, grad_bias1, grad_dec2
```

```python
import functools

import jax
import jax.numpy as jnp
from jax import lax
from jax.experimental import pallas as pl
from jax.experimental.pallas import tpu as pltpu
from jax.sharding import PartitionSpec as P

F32 = jnp.float32
BF16 = jnp.bfloat16
I32 = jnp.int32
VMEM_BYTES = 24 * 1024 * 1024


def iota(shape, dim):
    return lax.broadcasted_iota(I32, shape, dim)


def split_index(index, size):
    if size & (size - 1) == 0:
        return lax.shift_right_logical(index, size.bit_length() - 1), index & (size - 1)
    return lax.div(index, size), lax.rem(index, size)


def dot(a, b, dims=((1,), (0,))):
    return lax.dot_general(a, b, (dims, ((), ())), preferred_element_type=F32)


def exact_dot(a, ids, dims, ids_first):
    high = lax.shift_right_logical(ids, 8).astype(F32).astype(BF16)
    low = (ids & 255).astype(F32).astype(BF16)
    if ids_first:
        return dot(high, a, dims) * 256.0 + dot(low, a, dims)
    return dot(a, high, dims) * 256.0 + dot(a, low, dims)


def ones_where(mask):
    return jnp.where(mask, 1.0, 0.0).astype(BF16)


def as_column(ids, count):
    n, w = ids.shape
    rows = n * count
    source, _ = split_index(iota((rows, n), 0), count)
    picked = exact_dot(ones_where(source == iota((rows, n), 1)), ids, ((1,), (0,)), False)
    _, lane = split_index(iota((rows, w), 0), count)
    return jnp.sum(jnp.where(lane == iota((rows, w), 1), picked, 0.0), axis=1, keepdims=True).astype(I32)


def as_row(ids, count):
    n, w = ids.shape
    rows = n * count
    _, lane = split_index(iota((w, rows), 1), count)
    picked = exact_dot(ones_where(lane == iota((w, rows), 0)), ids, ((1,), (0,)), True)
    source, _ = split_index(iota((n, rows), 1), count)
    return jnp.sum(jnp.where(source == iota((n, rows), 0), picked, 0.0), axis=0, keepdims=True).astype(I32)


def row_to_column(row):
    size = row.shape[1]
    same = iota((size, size), 0) == iota((size, size), 1)
    return jnp.sum(jnp.where(same, row, 0.0), axis=1, keepdims=True)


def request_kernel(cap, owner_ref, local_ref, halo_ref, word_ref, place_ref):
    n = word_ref.shape[0]
    owner = jnp.concatenate([owner_ref[0:1, :], owner_ref[1:2, :]], axis=1)
    local = jnp.concatenate([local_ref[0:1, :], local_ref[1:2, :]], axis=1)
    ends = owner.shape[1]
    match = iota((n, ends), 0) == owner
    upto = ones_where(iota((ends, ends), 0) <= iota((ends, ends), 1))
    count = dot(ones_where(match), upto)
    slot = jnp.sum(jnp.where(match, count, 0.0), axis=0, keepdims=True).astype(I32) - 1
    place_ref[...] = owner * cap + slot
    at_slot = ones_where(iota((cap, ends), 0) == slot)
    wanted = jnp.where(match, local, 0)
    ids = exact_dot(at_slot, wanted, ((1,), (1,)), True).astype(I32)
    word_ref[...] = ids
    halo = halo_ref.shape[1]
    word_ref[:, :halo] = ids[:, :halo] + lax.shift_left(halo_ref[...], 16)


def inner_kernel(feats_ref, adj_ref, w_ref, b_ref, place_ref, label_ref, agg_ref, base_ref, place_col_ref, target_ref):
    feats = feats_ref[...]
    agg_ref[...] = dot(adj_ref[...], feats)
    base_ref[...] = dot(feats, w_ref[...]) + b_ref[...]
    place_col_ref[...] = row_to_column(place_ref[...].astype(F32)).astype(I32)
    target_ref[...] = row_to_column(label_ref[...].astype(F32))


def halo_kernel(cap, word_ref, history_ref, out_ref):
    ids = as_column(lax.shift_right_logical(word_ref[...], 16), cap)
    nodes = history_ref.shape[0]
    out_ref[...] = dot(ones_where(ids == iota((ids.shape[0], nodes), 1)), history_ref[...]).astype(BF16)


def embed_kernel(cap, word_ref, agg_ref, base_ref, halo_ref, adj_ref, w_ref, embed_ref, out_ref):
    agg = (agg_ref[...] + dot(adj_ref[...], halo_ref[...])).astype(BF16)
    embed = jnp.maximum(base_ref[...] + dot(agg, w_ref[...]), 0.0).astype(BF16)
    embed_ref[...] = embed
    ids = as_column(word_ref[...] & 65535, cap)
    out_ref[...] = dot(ones_where(ids == iota((ids.shape[0], embed.shape[0]), 1)), embed).astype(BF16)


def decode_kernel(
    ends_ref, place_ref, place_col_ref, target_ref, w1_ref, b1_ref, w2_ref,
    grads_ref, z_ref, d_pre_ref, aux_ref,
):
    slots = ends_ref.shape[0]
    ends = place_ref.shape[1]
    queries = ends // 2
    rows = dot(ones_where(place_col_ref[...] == iota((ends, slots), 1)), ends_ref[...])
    head, tail = rows[:queries], rows[queries:]
    z = (head * tail).astype(BF16)
    w1 = w1_ref[...]
    pre = dot(z, w1) + b1_ref[...]
    sig = jax.nn.sigmoid(pre)
    hidden = (pre * sig).astype(BF16).astype(F32)
    w2 = w2_ref[...].astype(F32)
    logit = jnp.sum(hidden * w2, axis=1, keepdims=True)
    dlogit = jax.nn.sigmoid(logit) - target_ref[...]
    d_pre = (dlogit * w2 * (sig * (1.0 + pre * (1.0 - sig)))).astype(BF16)
    dz = dot(d_pre, w1, ((1,), (1,)))
    grads = jnp.concatenate([dz * tail, dz * head], axis=0).astype(BF16)
    grads_ref[...] = dot(ones_where(iota((slots, ends), 0) == place_ref[...]), grads).astype(BF16)
    z_ref[...] = z
    d_pre_ref[...] = d_pre
    first = iota(aux_ref.shape, 0)
    bias = jnp.sum(d_pre.astype(F32), axis=0, keepdims=True)
    outer = jnp.sum(hidden * dlogit, axis=0, keepdims=True)
    aux_ref[...] = jnp.where(first == 0, bias, jnp.where(first == 1, outer, 0.0))


def weight_kernel(rep_ref, z_ref, d_pre_ref, aux_ref, keep_ref, send_ref):
    grad = dot(z_ref[...], d_pre_ref[...], ((0,), (0,)))
    half = grad.shape[0] // 2
    odd = (rep_ref[0] & 1) == 1
    low, high = grad[:half], grad[half:]
    keep_ref[:half] = jnp.where(odd, high, low)
    send_ref[:half] = jnp.where(odd, low, high)
    keep_ref[half:] = aux_ref[...]
    send_ref[half:] = aux_ref[...]


def scatter_kernel(cap, blocks, rep_ref, word_ref, grads_ref, keep_ref, send_ref):
    ids = as_row(word_ref[...] & 65535, cap)
    grads = grads_ref[...]
    size = keep_ref.shape[0] // (blocks // 2)
    for j in range(blocks):
        first = (rep_ref[0] ^ j) * size
        sums = dot(ones_where(iota((size, ids.shape[1]), 0) + first == ids), grads)
        out = send_ref if j % 2 else keep_ref
        out[(j // 2) * size:(j // 2 + 1) * size, :] = sums


def call(kernel, outs, *args, scalar=False):
    in_specs = [pl.BlockSpec(memory_space=pltpu.VMEM)] * len(args)
    if scalar:
        in_specs[0] = pl.BlockSpec(memory_space=pltpu.SMEM)
    return pl.pallas_call(
        kernel,
        out_shape=[jax.ShapeDtypeStruct(s, t) for s, t in outs],
        in_specs=in_specs,
        out_specs=[pl.BlockSpec(memory_space=pltpu.VMEM)] * len(outs),
        compiler_params=pltpu.CompilerParams(vmem_limit_bytes=VMEM_BYTES),
    )(*args)


def swap(x, axis, mask):
    return lax.ppermute(x, axis, [(i, i ^ mask) for i in range(lax.axis_size(axis))])


def exchange(x, axis):
    return lax.all_to_all(x, axis, split_axis=0, concat_axis=0, tiled=True)


def per_device(
    feats, history, adj_inner, adj_halo, halo_rows, w_self, w_nbr, b_enc,
    edge_owner, edge_rows, labels, w_dec1, b_dec1, w_dec2,
):
    n_dom = lax.axis_size("dom")
    n_rep = lax.axis_size("rep")
    nodes, width = feats.shape
    queries = edge_owner.shape[0]
    cap_halo = halo_rows.shape[1]
    cap = max(2, 4 * queries // n_dom)
    slots = n_dom * cap
    rep = lax.axis_index("rep").astype(I32).reshape(1)

    word, place = call(
        functools.partial(request_kernel, cap),
        [((n_dom, cap), I32), ((1, 2 * queries), I32)],
        edge_owner.T, edge_rows.T, halo_rows,
    )
    word = exchange(word, "dom")
    agg, base, place_col, target = call(
        inner_kernel,
        [((nodes, width), F32), ((nodes, width), F32), ((2 * queries, 1), I32), ((queries, 1), F32)],
        feats, adj_inner, w_self, b_enc.reshape(1, -1), place, labels.reshape(1, -1),
    )
    (halo,) = call(functools.partial(halo_kernel, cap_halo), [((n_dom * cap_halo, width), BF16)], word, history)
    halo = exchange(halo.reshape(n_dom, cap_halo, width), "dom").reshape(-1, width)
    embed, fetched = call(
        functools.partial(embed_kernel, cap),
        [((nodes, width), BF16), ((slots, width), BF16)],
        word, agg, base, halo, adj_halo, w_nbr,
    )
    fetched = exchange(fetched.reshape(n_dom, cap, width), "dom").reshape(-1, width)
    grads, z, d_pre, aux = call(
        decode_kernel,
        [((slots, width), BF16), ((queries, width), BF16), ((queries, width), BF16), ((8, width), F32)],
        fetched, place, place_col, target, w_dec1, b_dec1.reshape(1, -1), w_dec2.reshape(1, -1),
    )
    back = exchange(grads.reshape(n_dom, cap, width), "dom").reshape(-1, width)

    half = width // 2
    keep, send = call(
        weight_kernel, [((half + 8, width), F32), ((half + 8, width), F32)], rep, z, d_pre, aux, scalar=True
    )
    weights = keep + swap(send, "rep", 1)
    step = 2
    while step < n_rep:
        weights = weights + swap(weights, "rep", step)
        step *= 2
    step = 1
    while step < n_dom:
        weights = weights + swap(weights, "dom", step)
        step *= 2
    others = swap(weights, "rep", 1)

    size = nodes // n_rep
    keep, send = call(
        functools.partial(scatter_kernel, cap, n_rep),
        [((nodes // 2, width), F32), ((nodes // 2, width), F32)],
        rep, word, back, scalar=True,
    )
    sums = keep + swap(send, "rep", 1)
    step = 2
    while step < n_rep:
        blocks = sums.reshape(-1, 2, size, width)
        sums = blocks[:, 0] + swap(blocks[:, 1].astype(BF16), "rep", step).astype(F32)
        step *= 2
    grad_embed = sums.reshape(size, width)

    odd = (rep[0] & 1) == 1
    low = jnp.where(odd, others, weights)
    high = jnp.where(odd, weights, others)
    grad_dec1 = jnp.concatenate([low[:half], high[:half]], axis=0)
    return embed, grad_embed, grad_dec1, low[half], low[half + 1]


def solution(mesh):
    placed = (
        P("dom", None), P("dom", None), P("dom", None), P("dom", None), P("dom", None),
        P(), P(), P(),
        P(("dom", "rep"), None), P(("dom", "rep"), None), P(("dom", "rep")),
        P(), P(), P(),
    )
    return jax.shard_map(
        per_device,
        mesh=mesh,
        in_specs=placed,
        out_specs=(P("dom", None), P(("dom", "rep"), None), P(), P(), P()),
        check_vma=False,
    )
```

```python
import functools

import jax
import jax.numpy as jnp
from jax import lax
from jax.experimental import pallas as pl
from jax.experimental.pallas import tpu as pltpu
from jax.sharding import PartitionSpec as P

F32 = jnp.float32
BF16 = jnp.bfloat16
I32 = jnp.int32
VMEM_BYTES = 24 * 1024 * 1024
CHUNKS = 4


def iota(shape, dim):
    return lax.broadcasted_iota(I32, shape, dim)


def split_index(index, size):
    if size & (size - 1) == 0:
        return lax.shift_right_logical(index, size.bit_length() - 1), index & (size - 1)
    return lax.div(index, size), lax.rem(index, size)


def dot(a, b, dims=((1,), (0,))):
    return lax.dot_general(a, b, (dims, ((), ())), preferred_element_type=F32)


def exact_dot(a, ids, dims, ids_first):
    high = lax.shift_right_logical(ids, 8).astype(F32).astype(BF16)
    low = (ids & 255).astype(F32).astype(BF16)
    if ids_first:
        return dot(high, a, dims) * 256.0 + dot(low, a, dims)
    return dot(a, high, dims) * 256.0 + dot(a, low, dims)


def ones_where(mask):
    return jnp.where(mask, 1.0, 0.0).astype(BF16)


def as_column(ids, count):
    n, w = ids.shape
    rows = n * count
    source, _ = split_index(iota((rows, n), 0), count)
    picked = exact_dot(ones_where(source == iota((rows, n), 1)), ids, ((1,), (0,)), False)
    _, lane = split_index(iota((rows, w), 0), count)
    return jnp.sum(jnp.where(lane == iota((rows, w), 1), picked, 0.0), axis=1, keepdims=True).astype(I32)


def as_row(ids, count):
    n, w = ids.shape
    rows = n * count
    _, lane = split_index(iota((w, rows), 1), count)
    picked = exact_dot(ones_where(lane == iota((w, rows), 0)), ids, ((1,), (0,)), True)
    source, _ = split_index(iota((n, rows), 1), count)
    return jnp.sum(jnp.where(source == iota((n, rows), 0), picked, 0.0), axis=0, keepdims=True).astype(I32)


def row_to_column(row):
    size = row.shape[1]
    same = iota((size, size), 0) == iota((size, size), 1)
    return jnp.sum(jnp.where(same, row, 0.0), axis=1, keepdims=True)


def loads(sources, targets, sem):
    copies = [pltpu.make_async_copy(src, dst, sem.at[i]) for i, (src, dst) in enumerate(zip(sources, targets))]
    for copy in copies:
        copy.start()
    return copies


def wait(copies):
    for copy in copies:
        copy.wait()


def request_kernel(cap, owner_hbm, local_hbm, halo_hbm, word_ref, place_ref, owner_ref, local_ref, halo_ref, sem):
    wait(loads((owner_hbm, local_hbm, halo_hbm), (owner_ref, local_ref, halo_ref), sem))
    n = word_ref.shape[0]
    owner = jnp.concatenate([owner_ref[0:1, :], owner_ref[1:2, :]], axis=1)
    local = jnp.concatenate([local_ref[0:1, :], local_ref[1:2, :]], axis=1)
    ends = owner.shape[1]
    match = iota((n, ends), 0) == owner
    upto = ones_where(iota((ends, ends), 0) <= iota((ends, ends), 1))
    count = dot(ones_where(match), upto)
    slot = jnp.sum(jnp.where(match, count, 0.0), axis=0, keepdims=True).astype(I32) - 1
    place_ref[...] = owner * cap + slot
    at_slot = ones_where(iota((cap, ends), 0) == slot)
    wanted = jnp.where(match, local, 0)
    ids = exact_dot(at_slot, wanted, ((1,), (1,)), True).astype(I32)
    word_ref[...] = ids
    halo = halo_ref.shape[1]
    word_ref[:, :halo] = ids[:, :halo] + lax.shift_left(halo_ref[...], 16)


def store(value, buffer, out_ref, sem, chunks):
    rows = out_ref.shape[0] // chunks
    copies = []
    for j in range(chunks):
        at = pl.ds(j * rows, rows)
        buffer[at, :] = value(j * rows, rows)
        copy = pltpu.make_async_copy(buffer.at[at, :], out_ref.at[at, :], sem.at[j])
        copy.start()
        copies.append(copy)
    return copies


def load_kernel(history_hbm, history_ref, sem):
    wait(loads((history_hbm,), (history_ref,), sem))


def inner_kernel(
    cap, word_ref, feats_hbm, inner_hbm, self_hbm, b_hbm, halo_hbm, nbr_hbm,
    ids_ref, agg_ref, base_ref, halo_ref, nbr_ref, feats_ref, inner_ref, self_ref, b_ref, sem,
):
    copies = loads(
        (feats_hbm, inner_hbm, self_hbm, b_hbm, halo_hbm, nbr_hbm),
        (feats_ref, inner_ref, self_ref, b_ref, halo_ref, nbr_ref), sem,
    )
    ids_ref[...] = as_column(word_ref[...] & 65535, cap)
    wait(copies)
    feats = feats_ref[...]
    agg_ref[...] = dot(inner_ref[...], feats)
    base_ref[...] = dot(feats, self_ref[...]) + b_ref[...]


def edge_mask_kernel(
    place_ref, label_hbm, w1_hbm, b1_hbm, w2_hbm,
    gather_ref, scatter_ref, target_ref, w1_ref, b1_ref, w2_ref, label_ref, sem,
):
    copies = loads((label_hbm, w1_hbm, b1_hbm, w2_hbm), (label_ref, w1_ref, b1_ref, w2_ref), sem)
    place = place_ref[...]
    column = row_to_column(place.astype(F32)).astype(I32)
    gather_ref[...] = ones_where(column == iota(gather_ref.shape, 1))
    scatter_ref[...] = ones_where(iota(scatter_ref.shape, 0) == place)
    wait(copies)
    target_ref[...] = row_to_column(label_ref[...].astype(F32))


def sum_mask_kernel(cap, blocks, rep_ref, word_ref, mask_ref):
    ids = as_row(word_ref[...] & 65535, cap)
    size = mask_ref.shape[0] // blocks
    for j in range(blocks):
        node = iota((size, ids.shape[1]), 0) + (rep_ref[0] ^ j) * size
        mask_ref[j * size:(j + 1) * size, :] = ones_where(node == ids)


def halo_kernel(cap, word_ref, history_ref, out_ref):
    ids = as_column(lax.shift_right_logical(word_ref[...], 16), cap)
    nodes = history_ref.shape[0]
    out_ref[...] = dot(ones_where(ids == iota((ids.shape[0], nodes), 1)), history_ref[...]).astype(BF16)


def embed_kernel(ids_ref, agg_ref, base_ref, halo_ref, adj_ref, w_ref, embed_hbm, out_hbm, embed_ref, out_ref, embed_sem, out_sem):
    agg = (agg_ref[...] + dot(adj_ref[...], halo_ref[...])).astype(BF16)
    embed = jnp.maximum(base_ref[...] + dot(agg, w_ref[...]), 0.0).astype(BF16)
    copies = store(lambda at, size: embed[at:at + size], embed_ref, embed_hbm, embed_sem, 1)

    def fetched(at, size):
        mask = ones_where(ids_ref[at:at + size, :] == iota((size, embed.shape[0]), 1))
        return dot(mask, embed).astype(BF16)

    copies += store(fetched, out_ref, out_hbm, out_sem, CHUNKS)
    wait(copies)


def decode_kernel(
    rep_ref, ends_ref, gather_ref, target_ref, w1_ref, b1_ref, w2_ref, rows_ref, d_pre_ref, keep_ref, send_ref
):
    queries = d_pre_ref.shape[0]
    rows = dot(gather_ref[...], ends_ref[...])
    rows_ref[...] = rows.astype(BF16)
    z = (rows[:queries] * rows[queries:]).astype(BF16)
    pre = dot(z, w1_ref[...]) + b1_ref[...]
    sig = jax.nn.sigmoid(pre)
    hidden = (pre * sig).astype(BF16).astype(F32)
    w2 = w2_ref[...].astype(F32)
    logit = jnp.sum(hidden * w2, axis=1, keepdims=True)
    dlogit = jax.nn.sigmoid(logit) - target_ref[...]
    d_pre = (dlogit * w2 * (sig * (1.0 + pre * (1.0 - sig)))).astype(BF16)
    d_pre_ref[...] = d_pre
    grad = dot(z, d_pre, ((0,), (0,)))
    half = grad.shape[0] // 2
    odd = (rep_ref[0] & 1) == 1
    low, high = grad[:half], grad[half:]
    keep_ref[:half] = jnp.where(odd, high, low)
    send_ref[:half] = jnp.where(odd, low, high)
    bias = jnp.sum(d_pre.astype(F32), axis=0, keepdims=True)
    outer = jnp.sum(hidden * dlogit, axis=0, keepdims=True)
    first = iota((keep_ref.shape[0] - half, keep_ref.shape[1]), 0)
    aux = jnp.where(first == 0, bias, jnp.where(first == 1, outer, 0.0))
    keep_ref[half:] = aux
    send_ref[half:] = aux


def grads_kernel(rows_ref, d_pre_ref, w1_ref, scatter_ref, grads_hbm, grads_ref, sem):
    queries = d_pre_ref.shape[0]
    dz = dot(d_pre_ref[...], w1_ref[...], ((1,), (1,)))
    head, tail = rows_ref[:queries, :].astype(F32), rows_ref[queries:, :].astype(F32)
    grads = jnp.concatenate([dz * tail, dz * head], axis=0).astype(BF16)
    wait(store(lambda at, size: dot(scatter_ref[at:at + size, :], grads).astype(BF16), grads_ref, grads_hbm, sem, CHUNKS))


def join_kernel(rep_ref, mine_ref, other_ref, grad_ref, bias_ref, outer_ref):
    half = grad_ref.shape[0] // 2
    odd = (rep_ref[0] & 1) == 1
    mine, other = mine_ref[...], other_ref[...]
    low = jnp.where(odd, other, mine)
    grad_ref[:half] = low[:half]
    grad_ref[half:] = jnp.where(odd, mine, other)[:half]
    bias_ref[...] = low[half:half + 1]
    outer_ref[...] = low[half + 1:half + 2]


def scatter_kernel(size, mask_ref, grads_ref, keep_ref, send_ref):
    grads = grads_ref[...]
    for j in range(mask_ref.shape[0] // size):
        sums = dot(mask_ref[j * size:(j + 1) * size, :], grads)
        out = send_ref if j % 2 else keep_ref
        out[(j // 2) * size:(j // 2 + 1) * size, :] = sums


def call(kernel, outs, *args, scalar=False, hbm_in=(), hbm_out=(), far_out=(), scratch=()):
    far_out = tuple(far_out) + tuple(hbm_out)
    space = pl.BlockSpec(memory_space=pltpu.VMEM)
    far = pl.BlockSpec(memory_space=pltpu.HBM)
    in_specs = [far if i in hbm_in else space for i in range(len(args))]
    if scalar:
        in_specs[0] = pl.BlockSpec(memory_space=pltpu.SMEM)
    args = [pltpu.with_memory_space_constraint(x, pltpu.HBM) if i in hbm_in else x for i, x in enumerate(args)]
    return pl.pallas_call(
        kernel,
        out_shape=[(pltpu.HBM if i in far_out else pltpu.VMEM)(s, t) for i, (s, t) in enumerate(outs)],
        in_specs=in_specs,
        out_specs=[far if i in hbm_out else space for i in range(len(outs))],
        scratch_shapes=list(scratch),
        compiler_params=pltpu.CompilerParams(vmem_limit_bytes=VMEM_BYTES),
    )(*args)


def swap(x, axis, mask):
    return lax.ppermute(x, axis, [(i, i ^ mask) for i in range(lax.axis_size(axis))])


def reduce_pairs(x, axis, mask):
    mine = x.astype(BF16)
    return mine.astype(F32) + swap(mine, axis, mask).astype(F32)


def reduce_fours(x, axis, mask):
    mine = x.astype(BF16)
    first, second, third = (swap(mine, axis, mask * k).astype(F32) for k in (1, 2, 3))
    return (mine.astype(F32) + first) + (second + third)


def exchange(x, axis):
    return lax.all_to_all(x, axis, split_axis=0, concat_axis=0, tiled=True)


def per_device(
    feats, history, adj_inner, adj_halo, halo_rows, w_self, w_nbr, b_enc,
    edge_owner, edge_rows, labels, w_dec1, b_dec1, w_dec2,
):
    n_dom = lax.axis_size("dom")
    n_rep = lax.axis_size("rep")
    nodes, width = feats.shape
    queries = edge_owner.shape[0]
    cap_halo = halo_rows.shape[1]
    cap = max(2, 4 * queries // n_dom)
    slots = n_dom * cap
    rep = lax.axis_index("rep").astype(I32).reshape(1)

    ends = 2 * queries
    word, place = call(
        functools.partial(request_kernel, cap),
        [((n_dom, cap), I32), ((1, ends), I32)],
        edge_owner.T, edge_rows.T, halo_rows,
        far_out=(0,),
        hbm_in=(0, 1, 2),
        scratch=(
            pltpu.VMEM((2, queries), I32), pltpu.VMEM((2, queries), I32), pltpu.VMEM(halo_rows.shape, I32),
            pltpu.SemaphoreType.DMA((3,)),
        ),
    )
    word = exchange(word, "dom")
    (history,) = call(
        load_kernel, [(history.shape, BF16)], history, hbm_in=(0,), scratch=(pltpu.SemaphoreType.DMA((1,)),)
    )
    (halo,) = call(
        functools.partial(halo_kernel, cap_halo), [((n_dom * cap_halo, width), BF16)], word, history, far_out=(0,)
    )
    halo = exchange(halo.reshape(n_dom, cap_halo, width), "dom").reshape(-1, width)
    fetch, agg, base, adj_halo, w_nbr = call(
        functools.partial(inner_kernel, cap),
        [
            ((slots, 1), I32), ((nodes, width), F32), ((nodes, width), F32),
            (adj_halo.shape, BF16), (w_nbr.shape, BF16),
        ],
        word, feats, adj_inner, w_self, b_enc.reshape(1, -1), adj_halo, w_nbr,
        hbm_in=(1, 2, 3, 4, 5, 6),
        scratch=(
            pltpu.VMEM(feats.shape, BF16), pltpu.VMEM(adj_inner.shape, BF16), pltpu.VMEM(w_self.shape, BF16),
            pltpu.VMEM((1, width), F32), pltpu.SemaphoreType.DMA((6,)),
        ),
    )
    embed, fetched = call(
        embed_kernel,
        [((nodes, width), BF16), ((slots, width), BF16)],
        fetch, agg, base, halo, adj_halo, w_nbr,
        hbm_out=(0, 1),
        scratch=(
            pltpu.VMEM((nodes, width), BF16), pltpu.VMEM((slots, width), BF16),
            pltpu.SemaphoreType.DMA((1,)), pltpu.SemaphoreType.DMA((CHUNKS,)),
        ),
    )
    fetched = exchange(fetched.reshape(n_dom, cap, width), "dom").reshape(-1, width)
    gather, scatter, target, w1, b1, w2 = call(
        edge_mask_kernel,
        [
            ((ends, slots), BF16), ((slots, ends), BF16), ((queries, 1), F32),
            (w_dec1.shape, BF16), ((1, width), F32), ((1, width), BF16),
        ],
        place, labels.reshape(1, -1), w_dec1, b_dec1.reshape(1, -1), w_dec2.reshape(1, -1),
        hbm_in=(1, 2, 3, 4),
        scratch=(pltpu.VMEM((1, queries), I32), pltpu.SemaphoreType.DMA((4,))),
    )
    half = width // 2
    rows, d_pre, keep, send = call(
        decode_kernel,
        [((ends, width), BF16), ((queries, width), BF16), ((half + 8, width), F32), ((half + 8, width), F32)],
        rep, fetched, gather, target, w1, b1, w2, scalar=True,
    )
    weights = keep + swap(send, "rep", 1)
    step = 2
    while step < n_rep:
        weights = reduce_pairs(weights, "rep", step)
        step *= 2
    step = 1
    while 4 * step <= n_dom // 2:
        weights = reduce_fours(weights, "dom", step)
        step *= 4
    (grads,) = call(
        grads_kernel,
        [((slots, width), BF16)],
        rows, d_pre, w1, scatter,
        hbm_out=(0,),
        scratch=(pltpu.VMEM((slots, width), BF16), pltpu.SemaphoreType.DMA((CHUNKS,))),
    )
    back = exchange(grads.reshape(n_dom, cap, width), "dom").reshape(-1, width)

    back, weights = lax.optimization_barrier((back, weights))
    size = nodes // n_rep
    (mask,) = call(
        functools.partial(sum_mask_kernel, cap, n_rep), [((nodes, slots), BF16)], rep, word, scalar=True
    )
    keep, send = call(
        functools.partial(scatter_kernel, size),
        [((nodes // 2, width), F32), ((nodes // 2, width), F32)],
        mask, back,
    )
    sums = keep + swap(send, "rep", 1)
    rep_step = 2
    while rep_step < n_rep:
        blocks = sums.reshape(-1, 2, size, width)
        away = swap(blocks[:, 1].astype(BF16), "rep", rep_step)
        if step < n_dom:
            mine = weights.astype(BF16)
            others = swap(mine, "dom", step)
            others, away = lax.optimization_barrier((others, away))
            weights = mine.astype(F32) + others.astype(F32)
            step *= 2
        sums = blocks[:, 0] + away.astype(F32)
        rep_step *= 2
    grad_embed = sums.reshape(size, width)
    while step < n_dom:
        weights = reduce_pairs(weights, "dom", step)
        step *= 2

    others = swap(weights, "rep", 1)
    grad_dec1, grad_bias1, grad_dec2 = call(
        join_kernel,
        [((width, width), F32), ((1, width), F32), ((1, width), F32)],
        rep, weights, others, scalar=True, far_out=(0, 1, 2),
    )
    return embed, grad_embed, grad_dec1, grad_bias1[0], grad_dec2[0]


def solution(mesh):
    placed = (
        P("dom", None), P("dom", None), P("dom", None), P("dom", None), P("dom", None),
        P(), P(), P(),
        P(("dom", "rep"), None), P(("dom", "rep"), None), P(("dom", "rep")),
        P(), P(), P(),
    )
    return jax.shard_map(
        per_device,
        mesh=mesh,
        in_specs=placed,
        out_specs=(P("dom", None), P(("dom", "rep"), None), P(), P(), P()),
        check_vma=False,
    )
```

```python
import functools

import jax
import jax.numpy as jnp
from jax import lax
from jax.experimental import pallas as pl
from jax.experimental.pallas import tpu as pltpu
from jax.sharding import PartitionSpec as P

F32 = jnp.float32
BF16 = jnp.bfloat16
I32 = jnp.int32
VMEM_BYTES = 24 * 1024 * 1024
CHUNKS = 4
X_PARTS = 2


def iota(shape, dim):
    return lax.broadcasted_iota(I32, shape, dim)


def split_index(index, size):
    if size & (size - 1) == 0:
        return lax.shift_right_logical(index, size.bit_length() - 1), index & (size - 1)
    return lax.div(index, size), lax.rem(index, size)


def dot(a, b, dims=((1,), (0,))):
    return lax.dot_general(a, b, (dims, ((), ())), preferred_element_type=F32)


def exact_dot(a, ids, dims, ids_first):
    high = lax.shift_right_logical(ids, 8).astype(F32).astype(BF16)
    low = (ids & 255).astype(F32).astype(BF16)
    if ids_first:
        return dot(high, a, dims) * 256.0 + dot(low, a, dims)
    return dot(a, high, dims) * 256.0 + dot(a, low, dims)


def ones_where(mask):
    return jnp.where(mask, 1.0, 0.0).astype(BF16)


def as_column(ids, count):
    n, w = ids.shape
    rows = n * count
    source, _ = split_index(iota((rows, n), 0), count)
    picked = exact_dot(ones_where(source == iota((rows, n), 1)), ids, ((1,), (0,)), False)
    _, lane = split_index(iota((rows, w), 0), count)
    return jnp.sum(jnp.where(lane == iota((rows, w), 1), picked, 0.0), axis=1, keepdims=True).astype(I32)


def as_row(ids, count):
    n, w = ids.shape
    rows = n * count
    _, lane = split_index(iota((w, rows), 1), count)
    picked = exact_dot(ones_where(lane == iota((w, rows), 0)), ids, ((1,), (0,)), True)
    source, _ = split_index(iota((n, rows), 1), count)
    return jnp.sum(jnp.where(source == iota((n, rows), 0), picked, 0.0), axis=0, keepdims=True).astype(I32)


def row_to_column(row):
    size = row.shape[1]
    same = iota((size, size), 0) == iota((size, size), 1)
    return jnp.sum(jnp.where(same, row, 0.0), axis=1, keepdims=True)


def loads(sources, targets, sem):
    copies = [pltpu.make_async_copy(src, dst, sem.at[i]) for i, (src, dst) in enumerate(zip(sources, targets))]
    for copy in copies:
        copy.start()
    return copies


def wait(copies):
    for copy in copies:
        copy.wait()


def request_kernel(cap, owner_hbm, local_hbm, halo_hbm, word_ref, place_ref, owner_ref, local_ref, halo_ref, sem):
    wait(loads((owner_hbm, local_hbm, halo_hbm), (owner_ref, local_ref, halo_ref), sem))
    n = word_ref.shape[0]
    owner = jnp.concatenate([owner_ref[0:1, :], owner_ref[1:2, :]], axis=1)
    local = jnp.concatenate([local_ref[0:1, :], local_ref[1:2, :]], axis=1)
    ends = owner.shape[1]
    match = iota((n, ends), 0) == owner
    upto = ones_where(iota((ends, ends), 0) <= iota((ends, ends), 1))
    count = dot(ones_where(match), upto)
    slot = jnp.sum(jnp.where(match, count, 0.0), axis=0, keepdims=True).astype(I32) - 1
    place_ref[...] = owner * cap + slot
    at_slot = ones_where(iota((cap, ends), 0) == slot)
    wanted = jnp.where(match, local, 0)
    ids = exact_dot(at_slot, wanted, ((1,), (1,)), True).astype(I32)
    word_ref[...] = ids
    halo = halo_ref.shape[1]
    word_ref[:, :halo] = ids[:, :halo] + lax.shift_left(halo_ref[...], 16)


def store(value, buffer, out_ref, sem, chunks):
    rows = out_ref.shape[0] // chunks
    copies = []
    for j in range(chunks):
        at = pl.ds(j * rows, rows)
        buffer[at, :] = value(j * rows, rows)
        copy = pltpu.make_async_copy(buffer.at[at, :], out_ref.at[at, :], sem.at[j])
        copy.start()
        copies.append(copy)
    return copies


def inner_kernel(
    feats_hbm, inner_hbm, self_hbm, b_hbm, halo_hbm, nbr_hbm, history_hbm,
    agg_ref, base_ref, halo_ref, nbr_ref, history_ref, feats_ref, inner_ref, self_ref, b_ref, sem,
):
    copies = loads(
        (feats_hbm, inner_hbm, self_hbm, b_hbm, halo_hbm, nbr_hbm, history_hbm),
        (feats_ref, inner_ref, self_ref, b_ref, halo_ref, nbr_ref, history_ref), sem,
    )
    wait(copies)
    feats = feats_ref[...]
    agg_ref[...] = dot(inner_ref[...], feats)
    base_ref[...] = dot(feats, self_ref[...]) + b_ref[...]


def edge_mask_kernel(
    place_ref, label_hbm, w1_hbm, b1_hbm, w2_hbm,
    gather_ref, scatter_ref, target_ref, w1_ref, b1_ref, w2_ref, label_ref, sem,
):
    copies = loads((label_hbm, w1_hbm, b1_hbm, w2_hbm), (label_ref, w1_ref, b1_ref, w2_ref), sem)
    place = place_ref[...]
    column = row_to_column(place.astype(F32)).astype(I32)
    gather_ref[...] = ones_where(column == iota(gather_ref.shape, 1))
    scatter_ref[...] = ones_where(iota(scatter_ref.shape, 0) == place)
    wait(copies)
    target_ref[...] = row_to_column(label_ref[...].astype(F32))


def sum_mask_kernel(cap, rep_ref, word_ref, *mask_refs):
    ids = as_row(word_ref[...] & 65535, cap)
    size = mask_refs[0].shape[0]
    for j, mask_ref in enumerate(mask_refs):
        node = iota((size, ids.shape[1]), 0) + (rep_ref[0] ^ j) * size
        mask_ref[...] = ones_where(node == ids)


def halo_kernel(cap, cap_edge, word_ref, history_ref, out_ref, ids_ref):
    ids_ref[...] = as_column(word_ref[...] & 65535, cap_edge)
    ids = as_column(lax.shift_right_logical(word_ref[...], 16), cap)
    nodes = history_ref.shape[0]
    out_ref[...] = dot(ones_where(ids == iota((ids.shape[0], nodes), 1)), history_ref[...]).astype(BF16)


def embed_kernel(ids_ref, agg_ref, base_ref, halo_ref, adj_ref, w_ref, embed_hbm, out_hbm, embed_ref, out_ref, embed_sem, out_sem):
    agg = (agg_ref[...] + dot(adj_ref[...], halo_ref[...])).astype(BF16)
    embed = jnp.maximum(base_ref[...] + dot(agg, w_ref[...]), 0.0).astype(BF16)
    copies = store(lambda at, size: embed[at:at + size], embed_ref, embed_hbm, embed_sem, 1)

    def fetched(at, size):
        mask = ones_where(ids_ref[at:at + size, :] == iota((size, embed.shape[0]), 1))
        return dot(mask, embed).astype(BF16)

    copies += store(fetched, out_ref, out_hbm, out_sem, CHUNKS)
    wait(copies)


def decode_kernel(
    rep_ref, ends_ref, gather_ref, target_ref, w1_ref, b1_ref, w2_ref, rows_ref, d_pre_ref, keep_ref, send_ref
):
    queries = d_pre_ref.shape[0]
    rows = dot(gather_ref[...], ends_ref[...])
    rows_ref[...] = rows.astype(BF16)
    z = (rows[:queries] * rows[queries:]).astype(BF16)
    pre = dot(z, w1_ref[...]) + b1_ref[...]
    sig = jax.nn.sigmoid(pre)
    hidden = (pre * sig).astype(BF16).astype(F32)
    w2 = w2_ref[...].astype(F32)
    logit = jnp.sum(hidden * w2, axis=1, keepdims=True)
    dlogit = jax.nn.sigmoid(logit) - target_ref[...]
    d_pre = (dlogit * w2 * (sig * (1.0 + pre * (1.0 - sig)))).astype(BF16)
    d_pre_ref[...] = d_pre
    grad = dot(z, d_pre, ((0,), (0,)))
    half = grad.shape[0] // 2
    odd = (rep_ref[0] & 1) == 1
    low, high = grad[:half], grad[half:]
    keep_ref[:half] = jnp.where(odd, high, low)
    send_ref[:half] = jnp.where(odd, low, high)
    bias = jnp.sum(d_pre.astype(F32), axis=0, keepdims=True)
    outer = jnp.sum(hidden * dlogit, axis=0, keepdims=True)
    first = iota((keep_ref.shape[0] - half, keep_ref.shape[1]), 0)
    aux = jnp.where(first == 0, bias, jnp.where(first == 1, outer, 0.0))
    keep_ref[half:] = aux
    send_ref[half:] = aux


def grads_kernel(rows_ref, d_pre_ref, w1_ref, grads_ref):
    queries = d_pre_ref.shape[0]
    dz = dot(d_pre_ref[...], w1_ref[...], ((1,), (1,)))
    grads_ref[:queries, :] = (dz * rows_ref[queries:, :].astype(F32)).astype(BF16)
    grads_ref[queries:, :] = (dz * rows_ref[:queries, :].astype(F32)).astype(BF16)


def place_kernel(grads_ref, scatter_ref, out_hbm, out_ref, sem):
    grads = grads_ref[...]
    wait(store(lambda at, size: dot(scatter_ref[at:at + size, :], grads).astype(BF16), out_ref, out_hbm, sem, CHUNKS))


def final_kernel(rep_ref, mine_ref, other_ref, keep_ref, *refs):
    away_refs, (sums_ref, grad_ref, bias_ref, outer_ref) = refs[:-4], refs[-4:]
    rows = keep_ref.shape[0] // max(1, len(away_refs))
    for i, away_ref in enumerate(away_refs):
        at = pl.ds(i * rows, rows)
        sums_ref[at, :] = keep_ref[at, :] + away_ref[...].astype(F32)
    if not away_refs:
        sums_ref[...] = keep_ref[...]
    half = grad_ref.shape[0] // 2
    odd = (rep_ref[0] & 1) == 1
    mine, other = mine_ref[...], other_ref[...]
    low = jnp.where(odd, other, mine)
    grad_ref[:half] = low[:half]
    grad_ref[half:] = jnp.where(odd, mine, other)[:half]
    bias_ref[...] = low[half:half + 1]
    outer_ref[...] = low[half + 1:half + 2]


def scatter_kernel(mask_ref, grads_ref, out_ref):
    out_ref[...] = dot(mask_ref[...], grads_ref[...]).astype(out_ref.dtype)


def call(kernel, outs, *args, scalar=False, hbm_in=(), hbm_out=(), far_out=(), scratch=()):
    far_out = tuple(far_out) + tuple(hbm_out)
    space = pl.BlockSpec(memory_space=pltpu.VMEM)
    far = pl.BlockSpec(memory_space=pltpu.HBM)
    in_specs = [far if i in hbm_in else space for i in range(len(args))]
    if scalar:
        in_specs[0] = pl.BlockSpec(memory_space=pltpu.SMEM)
    args = [pltpu.with_memory_space_constraint(x, pltpu.HBM) if i in hbm_in else x for i, x in enumerate(args)]
    return pl.pallas_call(
        kernel,
        out_shape=[(pltpu.HBM if i in far_out else pltpu.VMEM)(s, t) for i, (s, t) in enumerate(outs)],
        in_specs=in_specs,
        out_specs=[far if i in hbm_out else space for i in range(len(outs))],
        scratch_shapes=list(scratch),
        compiler_params=pltpu.CompilerParams(vmem_limit_bytes=VMEM_BYTES),
    )(*args)


def swap(x, axis, mask):
    return lax.ppermute(x, axis, [(i, i ^ mask) for i in range(lax.axis_size(axis))])


def reduce_pairs(x, axis, mask):
    mine = x.astype(BF16)
    return mine.astype(F32) + swap(mine, axis, mask).astype(F32)


def reduce_fours(x, axis, mask):
    mine = x.astype(BF16)
    first, second, third = (swap(mine, axis, mask * k).astype(F32) for k in (1, 2, 3))
    return (mine.astype(F32) + first) + (second + third)


def exchange(x, axis):
    return lax.all_to_all(x, axis, split_axis=0, concat_axis=0, tiled=True)


def per_device(
    feats, history, adj_inner, adj_halo, halo_rows, w_self, w_nbr, b_enc,
    edge_owner, edge_rows, labels, w_dec1, b_dec1, w_dec2,
):
    n_dom = lax.axis_size("dom")
    n_rep = lax.axis_size("rep")
    nodes, width = feats.shape
    queries = edge_owner.shape[0]
    cap_halo = halo_rows.shape[1]
    cap = max(2, 4 * queries // n_dom)
    slots = n_dom * cap
    rep = lax.axis_index("rep").astype(I32).reshape(1)

    ends = 2 * queries
    word, place = call(
        functools.partial(request_kernel, cap),
        [((n_dom, cap), I32), ((1, ends), I32)],
        edge_owner.T, edge_rows.T, halo_rows,
        far_out=(0,),
        hbm_in=(0, 1, 2),
        scratch=(
            pltpu.VMEM((2, queries), I32), pltpu.VMEM((2, queries), I32), pltpu.VMEM(halo_rows.shape, I32),
            pltpu.SemaphoreType.DMA((3,)),
        ),
    )
    word = exchange(word, "dom")
    agg, base, adj_halo, w_nbr, history = call(
        inner_kernel,
        [
            ((nodes, width), F32), ((nodes, width), F32),
            (adj_halo.shape, BF16), (w_nbr.shape, BF16), (history.shape, BF16),
        ],
        feats, adj_inner, w_self, b_enc.reshape(1, -1), adj_halo, w_nbr, history,
        hbm_in=(0, 1, 2, 3, 4, 5, 6),
        scratch=(
            pltpu.VMEM(feats.shape, BF16), pltpu.VMEM(adj_inner.shape, BF16), pltpu.VMEM(w_self.shape, BF16),
            pltpu.VMEM((1, width), F32), pltpu.SemaphoreType.DMA((7,)),
        ),
    )
    halo, ids = call(
        functools.partial(halo_kernel, cap_halo, cap),
        [((n_dom * cap_halo, width), BF16), ((slots, 1), I32)],
        word, history,
    )
    halo = exchange(halo.reshape(n_dom, cap_halo, width), "dom").reshape(-1, width)
    embed, fetched = call(
        embed_kernel,
        [((nodes, width), BF16), ((slots, width), BF16)],
        ids, agg, base, halo, adj_halo, w_nbr,
        hbm_out=(0, 1),
        scratch=(
            pltpu.VMEM((nodes, width), BF16), pltpu.VMEM((slots, width), BF16),
            pltpu.SemaphoreType.DMA((1,)), pltpu.SemaphoreType.DMA((CHUNKS,)),
        ),
    )
    fetched = exchange(fetched.reshape(n_dom, cap, width), "dom").reshape(-1, width)
    gather, scatter, target, w1, b1, w2 = call(
        edge_mask_kernel,
        [
            ((ends, slots), BF16), ((slots, ends), BF16), ((queries, 1), F32),
            (w_dec1.shape, BF16), ((1, width), F32), ((1, width), BF16),
        ],
        place, labels.reshape(1, -1), w_dec1, b_dec1.reshape(1, -1), w_dec2.reshape(1, -1),
        hbm_in=(1, 2, 3, 4),
        scratch=(pltpu.VMEM((1, queries), I32), pltpu.SemaphoreType.DMA((4,))),
    )
    half = width // 2
    rows, d_pre, keep, send = call(
        decode_kernel,
        [((ends, width), BF16), ((queries, width), BF16), ((half + 8, width), F32), ((half + 8, width), F32)],
        rep, fetched, gather, target, w1, b1, w2, scalar=True,
    )
    weights = keep + swap(send, "rep", 1)
    (grads,) = call(grads_kernel, [((ends, width), BF16)], rows, d_pre, w1)
    grads, weights = lax.optimization_barrier((grads, weights))
    step = 2
    while step < n_rep:
        weights = reduce_pairs(weights, "rep", step)
        step *= 2
    (placed,) = call(
        place_kernel,
        [((slots, width), BF16)],
        grads, scatter,
        hbm_out=(0,),
        scratch=(pltpu.VMEM((slots, width), BF16), pltpu.SemaphoreType.DMA((CHUNKS,))),
    )
    back = exchange(placed.reshape(n_dom, cap, width), "dom").reshape(-1, width)
    step = 1
    while 4 * step <= n_dom // 2:
        weights = reduce_fours(weights, "dom", step)
        step *= 4

    back, weights = lax.optimization_barrier((back, weights))
    size = nodes // n_rep
    masks = call(
        functools.partial(sum_mask_kernel, cap), [((size, slots), BF16)] * n_rep, rep, word, scalar=True
    )

    def block_sum(j, dtype):
        (out,) = call(scatter_kernel, [((size, width), dtype)], masks[j], back)
        return out

    sums = {}
    for j in reversed(range(0, n_rep, 2)):
        send = block_sum(j + 1, BF16)
        sums[j] = block_sum(j, F32) + swap(send, "rep", 1).astype(F32)
    rep_step, away = 2, []
    while rep_step < n_rep:
        for j in range(0, n_rep, 2 * rep_step):
            parts = jnp.split(sums[j + rep_step].astype(BF16), X_PARTS, axis=0)
            away = [swap(part, "rep", rep_step) for part in parts]
            if step < n_dom:
                mine = weights.astype(BF16)
                others = swap(mine, "dom", step)
                others, away[0] = lax.optimization_barrier((others, away[0]))
                weights = mine.astype(F32) + others.astype(F32)
                step *= 2
            if 2 * rep_step < n_rep:
                sums[j] = sums[j] + jnp.concatenate(away, axis=0).astype(F32)
        rep_step *= 2
    while step < n_dom:
        weights = reduce_pairs(weights, "dom", step)
        step *= 2

    others = swap(weights, "rep", 1)
    grad_embed, grad_dec1, grad_bias1, grad_dec2 = call(
        final_kernel,
        [((size, width), F32), ((width, width), F32), ((1, width), F32), ((1, width), F32)],
        rep, weights, others, sums[0], *away, scalar=True, far_out=(0, 1, 2, 3),
    )
    return embed, grad_embed, grad_dec1, grad_bias1[0], grad_dec2[0]


def solution(mesh):
    placed = (
        P("dom", None), P("dom", None), P("dom", None), P("dom", None), P("dom", None),
        P(), P(), P(),
        P(("dom", "rep"), None), P(("dom", "rep"), None), P(("dom", "rep")),
        P(), P(), P(),
    )
    return jax.shard_map(
        per_device,
        mesh=mesh,
        in_specs=placed,
        out_specs=(P("dom", None), P(("dom", "rep"), None), P(), P(), P()),
        check_vma=False,
    )
```

```python
import functools

import jax
import jax.numpy as jnp
from jax import lax
from jax.experimental import pallas as pl
from jax.experimental.pallas import tpu as pltpu
from jax.sharding import PartitionSpec as P

F32 = jnp.float32
BF16 = jnp.bfloat16
I32 = jnp.int32
VMEM_BYTES = 24 * 1024 * 1024
CHUNKS = 4
X_PARTS = 2


def iota(shape, dim):
    return lax.broadcasted_iota(I32, shape, dim)


def split_index(index, size):
    if size & (size - 1) == 0:
        return lax.shift_right_logical(index, size.bit_length() - 1), index & (size - 1)
    return lax.div(index, size), lax.rem(index, size)


def dot(a, b, dims=((1,), (0,))):
    return lax.dot_general(a, b, (dims, ((), ())), preferred_element_type=F32)


def exact_dot(a, ids, dims, ids_first):
    high = lax.shift_right_logical(ids, 8).astype(F32).astype(BF16)
    low = (ids & 255).astype(F32).astype(BF16)
    if ids_first:
        return dot(high, a, dims) * 256.0 + dot(low, a, dims)
    return dot(a, high, dims) * 256.0 + dot(a, low, dims)


def ones_where(mask):
    return jnp.where(mask, 1.0, 0.0).astype(BF16)


def as_column(ids, count):
    n, w = ids.shape
    rows = n * count
    source, _ = split_index(iota((rows, n), 0), count)
    picked = exact_dot(ones_where(source == iota((rows, n), 1)), ids, ((1,), (0,)), False)
    _, lane = split_index(iota((rows, w), 0), count)
    return jnp.sum(jnp.where(lane == iota((rows, w), 1), picked, 0.0), axis=1, keepdims=True).astype(I32)


def as_row(ids, count):
    n, w = ids.shape
    rows = n * count
    _, lane = split_index(iota((w, rows), 1), count)
    picked = exact_dot(ones_where(lane == iota((w, rows), 0)), ids, ((1,), (0,)), True)
    source, _ = split_index(iota((n, rows), 1), count)
    return jnp.sum(jnp.where(source == iota((n, rows), 0), picked, 0.0), axis=0, keepdims=True).astype(I32)


def row_to_column(row):
    size = row.shape[1]
    same = iota((size, size), 0) == iota((size, size), 1)
    return jnp.sum(jnp.where(same, row, 0.0), axis=1, keepdims=True)


def loads(sources, targets, sem):
    copies = [pltpu.make_async_copy(src, dst, sem.at[i]) for i, (src, dst) in enumerate(zip(sources, targets))]
    for copy in copies:
        copy.start()
    return copies


def wait(copies):
    for copy in copies:
        copy.wait()


def request_kernel(cap, owner_hbm, local_hbm, halo_hbm, word_ref, place_ref, owner_ref, local_ref, halo_ref, sem):
    wait(loads((owner_hbm, local_hbm, halo_hbm), (owner_ref, local_ref, halo_ref), sem))
    n = word_ref.shape[0]
    owner = jnp.concatenate([owner_ref[0:1, :], owner_ref[1:2, :]], axis=1)
    local = jnp.concatenate([local_ref[0:1, :], local_ref[1:2, :]], axis=1)
    ends = owner.shape[1]
    match = iota((n, ends), 0) == owner
    upto = ones_where(iota((ends, ends), 0) <= iota((ends, ends), 1))
    count = dot(ones_where(match), upto)
    slot = jnp.sum(jnp.where(match, count, 0.0), axis=0, keepdims=True).astype(I32) - 1
    place_ref[...] = owner * cap + slot
    at_slot = ones_where(iota((cap, ends), 0) == slot)
    wanted = jnp.where(match, local, 0)
    ids = exact_dot(at_slot, wanted, ((1,), (1,)), True).astype(I32)
    word_ref[...] = ids
    halo = halo_ref.shape[1]
    word_ref[:, :halo] = ids[:, :halo] + lax.shift_left(halo_ref[...], 16)


def store(value, buffer, out_ref, sem, chunks):
    rows = out_ref.shape[0] // chunks
    copies = []
    for j in range(chunks):
        at = pl.ds(j * rows, rows)
        buffer[at, :] = value(j * rows, rows)
        copy = pltpu.make_async_copy(buffer.at[at, :], out_ref.at[at, :], sem.at[j])
        copy.start()
        copies.append(copy)
    return copies


def inner_kernel(
    feats_hbm, inner_hbm, self_hbm, b_hbm, halo_hbm, nbr_hbm, history_hbm,
    agg_ref, base_ref, halo_ref, nbr_ref, history_ref, feats_ref, inner_ref, self_ref, b_ref, sem,
):
    copies = loads(
        (feats_hbm, inner_hbm, self_hbm, b_hbm, halo_hbm, nbr_hbm, history_hbm),
        (feats_ref, inner_ref, self_ref, b_ref, halo_ref, nbr_ref, history_ref), sem,
    )
    wait(copies)
    feats = feats_ref[...]
    agg_ref[...] = dot(inner_ref[...], feats)
    base_ref[...] = dot(feats, self_ref[...]) + b_ref[...]


def edge_mask_kernel(
    place_ref, label_hbm, w1_hbm, b1_hbm, w2_hbm,
    gather_ref, scatter_ref, target_ref, w1_ref, b1_ref, w2_ref, label_ref, sem,
):
    copies = loads((label_hbm, w1_hbm, b1_hbm, w2_hbm), (label_ref, w1_ref, b1_ref, w2_ref), sem)
    place = place_ref[...]
    column = row_to_column(place.astype(F32)).astype(I32)
    gather_ref[...] = ones_where(column == iota(gather_ref.shape, 1))
    scatter_ref[...] = ones_where(iota(scatter_ref.shape, 0) == place)
    wait(copies)
    target_ref[...] = row_to_column(label_ref[...].astype(F32))


def sum_mask_kernel(cap, rep_ref, word_ref, *mask_refs):
    ids = as_row(word_ref[...] & 65535, cap)
    size = mask_refs[0].shape[0]
    for j, mask_ref in enumerate(mask_refs):
        node = iota((size, ids.shape[1]), 0) + (rep_ref[0] ^ j) * size
        mask_ref[...] = ones_where(node == ids)


def halo_kernel(cap, cap_edge, word_ref, history_ref, out_ref, ids_ref):
    ids_ref[...] = as_column(word_ref[...] & 65535, cap_edge)
    ids = as_column(lax.shift_right_logical(word_ref[...], 16), cap)
    nodes = history_ref.shape[0]
    out_ref[...] = dot(ones_where(ids == iota((ids.shape[0], nodes), 1)), history_ref[...]).astype(BF16)


def embed_kernel(ids_ref, agg_ref, base_ref, halo_ref, adj_ref, w_ref, embed_hbm, out_hbm, embed_ref, out_ref, embed_sem, out_sem):
    agg = (agg_ref[...] + dot(adj_ref[...], halo_ref[...])).astype(BF16)
    embed = jnp.maximum(base_ref[...] + dot(agg, w_ref[...]), 0.0).astype(BF16)
    copies = store(lambda at, size: embed[at:at + size], embed_ref, embed_hbm, embed_sem, 1)

    def fetched(at, size):
        mask = ones_where(ids_ref[at:at + size, :] == iota((size, embed.shape[0]), 1))
        return dot(mask, embed).astype(BF16)

    copies += store(fetched, out_ref, out_hbm, out_sem, CHUNKS)
    wait(copies)


def decode_kernel(
    rep_ref, ends_ref, gather_ref, scatter_ref, target_ref, w1_ref, b1_ref, w2_ref,
    grads_hbm, weights_ref, grads_ref, sem,
):
    rows = dot(gather_ref[...], ends_ref[...])
    queries = rows.shape[0] // 2
    head, tail = rows[:queries], rows[queries:]
    z = (head * tail).astype(BF16)
    w1 = w1_ref[...]
    pre = dot(z, w1) + b1_ref[...]
    sig = jax.nn.sigmoid(pre)
    hidden = (pre * sig).astype(BF16).astype(F32)
    w2 = w2_ref[...].astype(F32)
    logit = jnp.sum(hidden * w2, axis=1, keepdims=True)
    dlogit = jax.nn.sigmoid(logit) - target_ref[...]
    d_pre = (dlogit * w2 * (sig * (1.0 + pre * (1.0 - sig)))).astype(BF16)
    dz = dot(d_pre, w1, ((1,), (1,)))
    grads = jnp.concatenate([dz * tail, dz * head], axis=0).astype(BF16)
    copies = store(
        lambda at, size: dot(scatter_ref[at:at + size, :], grads).astype(BF16), grads_ref, grads_hbm, sem, CHUNKS
    )
    grad = dot(z, d_pre, ((0,), (0,)))
    half = grad.shape[0] // 2
    odd = (rep_ref[0] & 1) == 1
    low, high = grad[:half], grad[half:]
    bias = jnp.sum(d_pre.astype(F32), axis=0, keepdims=True)
    outer = jnp.sum(hidden * dlogit, axis=0, keepdims=True)
    first = iota((weights_ref.shape[0] // 2 - half, grad.shape[1]), 0)
    aux = jnp.where(first == 0, bias, jnp.where(first == 1, outer, 0.0))
    weights_ref[...] = jnp.concatenate([jnp.where(odd, high, low), aux, jnp.where(odd, low, high), aux], axis=0)
    wait(copies)


def final_kernel(rep_ref, mine_ref, other_ref, keep_ref, *refs):
    away_refs, (sums_ref, grad_ref, bias_ref, outer_ref) = refs[:-4], refs[-4:]
    rows = keep_ref.shape[0] // max(1, len(away_refs))
    for i, away_ref in enumerate(away_refs):
        at = pl.ds(i * rows, rows)
        sums_ref[at, :] = keep_ref[at, :] + away_ref[...].astype(F32)
    if not away_refs:
        sums_ref[...] = keep_ref[...]
    half = grad_ref.shape[0] // 2
    odd = (rep_ref[0] & 1) == 1
    mine, other = mine_ref[...], other_ref[...]
    low = jnp.where(odd, other, mine)
    grad_ref[:half] = low[:half]
    grad_ref[half:] = jnp.where(odd, mine, other)[:half]
    bias_ref[...] = low[half:half + 1]
    outer_ref[...] = low[half + 1:half + 2]


def scatter_kernel(mask_ref, grads_ref, out_ref):
    out_ref[...] = dot(mask_ref[...], grads_ref[...]).astype(out_ref.dtype)


def call(kernel, outs, *args, scalar=False, hbm_in=(), hbm_out=(), far_out=(), scratch=()):
    far_out = tuple(far_out) + tuple(hbm_out)
    space = pl.BlockSpec(memory_space=pltpu.VMEM)
    far = pl.BlockSpec(memory_space=pltpu.HBM)
    in_specs = [far if i in hbm_in else space for i in range(len(args))]
    if scalar:
        in_specs[0] = pl.BlockSpec(memory_space=pltpu.SMEM)
    args = [pltpu.with_memory_space_constraint(x, pltpu.HBM) if i in hbm_in else x for i, x in enumerate(args)]
    return pl.pallas_call(
        kernel,
        out_shape=[(pltpu.HBM if i in far_out else pltpu.VMEM)(s, t) for i, (s, t) in enumerate(outs)],
        in_specs=in_specs,
        out_specs=[far if i in hbm_out else space for i in range(len(outs))],
        scratch_shapes=list(scratch),
        compiler_params=pltpu.CompilerParams(vmem_limit_bytes=VMEM_BYTES),
    )(*args)


def swap(x, axis, mask):
    return lax.ppermute(x, axis, [(i, i ^ mask) for i in range(lax.axis_size(axis))])


def reduce_pairs(x, axis, mask):
    mine = x.astype(BF16)
    return mine.astype(F32) + swap(mine, axis, mask).astype(F32)


def reduce_fours(x, axis, mask):
    mine = x.astype(BF16)
    first, second, third = (swap(mine, axis, mask * k).astype(F32) for k in (1, 2, 3))
    return (mine.astype(F32) + first) + (second + third)


def exchange(x, axis):
    return lax.all_to_all(x, axis, split_axis=0, concat_axis=0, tiled=True)


def per_device(
    feats, history, adj_inner, adj_halo, halo_rows, w_self, w_nbr, b_enc,
    edge_owner, edge_rows, labels, w_dec1, b_dec1, w_dec2,
):
    n_dom = lax.axis_size("dom")
    n_rep = lax.axis_size("rep")
    nodes, width = feats.shape
    queries = edge_owner.shape[0]
    cap_halo = halo_rows.shape[1]
    cap = max(2, 4 * queries // n_dom)
    slots = n_dom * cap
    rep = lax.axis_index("rep").astype(I32).reshape(1)

    ends = 2 * queries
    word, place = call(
        functools.partial(request_kernel, cap),
        [((n_dom, cap), I32), ((1, ends), I32)],
        edge_owner.T, edge_rows.T, halo_rows,
        far_out=(0,),
        hbm_in=(0, 1, 2),
        scratch=(
            pltpu.VMEM((2, queries), I32), pltpu.VMEM((2, queries), I32), pltpu.VMEM(halo_rows.shape, I32),
            pltpu.SemaphoreType.DMA((3,)),
        ),
    )
    word = exchange(word, "dom")
    agg, base, adj_halo, w_nbr, history = call(
        inner_kernel,
        [
            ((nodes, width), F32), ((nodes, width), F32),
            (adj_halo.shape, BF16), (w_nbr.shape, BF16), (history.shape, BF16),
        ],
        feats, adj_inner, w_self, b_enc.reshape(1, -1), adj_halo, w_nbr, history,
        hbm_in=(0, 1, 2, 3, 4, 5, 6),
        scratch=(
            pltpu.VMEM(feats.shape, BF16), pltpu.VMEM(adj_inner.shape, BF16), pltpu.VMEM(w_self.shape, BF16),
            pltpu.VMEM((1, width), F32), pltpu.SemaphoreType.DMA((7,)),
        ),
    )
    halo, ids = call(
        functools.partial(halo_kernel, cap_halo, cap),
        [((n_dom * cap_halo, width), BF16), ((slots, 1), I32)],
        word, history,
    )
    halo = exchange(halo.reshape(n_dom, cap_halo, width), "dom").reshape(-1, width)
    embed, fetched = call(
        embed_kernel,
        [((nodes, width), BF16), ((slots, width), BF16)],
        ids, agg, base, halo, adj_halo, w_nbr,
        hbm_out=(0, 1),
        scratch=(
            pltpu.VMEM((nodes, width), BF16), pltpu.VMEM((slots, width), BF16),
            pltpu.SemaphoreType.DMA((1,)), pltpu.SemaphoreType.DMA((CHUNKS,)),
        ),
    )
    fetched = exchange(fetched.reshape(n_dom, cap, width), "dom").reshape(-1, width)
    gather, scatter, target, w1, b1, w2 = call(
        edge_mask_kernel,
        [
            ((ends, slots), BF16), ((slots, ends), BF16), ((queries, 1), F32),
            (w_dec1.shape, BF16), ((1, width), F32), ((1, width), BF16),
        ],
        place, labels.reshape(1, -1), w_dec1, b_dec1.reshape(1, -1), w_dec2.reshape(1, -1),
        hbm_in=(1, 2, 3, 4),
        scratch=(pltpu.VMEM((1, queries), I32), pltpu.SemaphoreType.DMA((4,))),
    )
    half = width // 2
    placed, weights = call(
        decode_kernel,
        [((slots, width), BF16), ((2 * (half + 8), width), F32)],
        rep, fetched, gather, scatter, target, w1, b1, w2,
        scalar=True,
        hbm_out=(0,),
        scratch=(pltpu.VMEM((slots, width), BF16), pltpu.SemaphoreType.DMA((CHUNKS,))),
    )
    back = exchange(placed.reshape(n_dom, cap, width), "dom").reshape(-1, width)
    step = 2
    while step < n_rep:
        weights = reduce_pairs(weights, "rep", step)
        step *= 2
    keep, send = jnp.split(weights, 2, axis=0)
    weights = keep + swap(send, "rep", 1)
    step = 1
    while 4 * step <= n_dom // 2:
        weights = reduce_fours(weights, "dom", step)
        step *= 4

    back, weights = lax.optimization_barrier((back, weights))
    size = nodes // n_rep
    masks = call(
        functools.partial(sum_mask_kernel, cap), [((size, slots), BF16)] * n_rep, rep, word, scalar=True
    )

    def block_sum(j, dtype):
        (out,) = call(scatter_kernel, [((size, width), dtype)], masks[j], back)
        return out

    sums = {}
    for j in reversed(range(0, n_rep, 2)):
        send = block_sum(j + 1, BF16)
        sums[j] = block_sum(j, F32) + swap(send, "rep", 1).astype(F32)
    rep_step, away = 2, []
    while rep_step < n_rep:
        for j in range(0, n_rep, 2 * rep_step):
            parts = jnp.split(sums[j + rep_step].astype(BF16), X_PARTS, axis=0)
            away = [swap(part, "rep", rep_step) for part in parts]
            if step < n_dom:
                mine = weights.astype(BF16)
                others = swap(mine, "dom", step)
                others, away[0] = lax.optimization_barrier((others, away[0]))
                weights = mine.astype(F32) + others.astype(F32)
                step *= 2
            if 2 * rep_step < n_rep:
                sums[j] = sums[j] + jnp.concatenate(away, axis=0).astype(F32)
        rep_step *= 2
    while step < n_dom:
        weights = reduce_pairs(weights, "dom", step)
        step *= 2

    others = swap(weights, "rep", 1)
    grad_embed, grad_dec1, grad_bias1, grad_dec2 = call(
        final_kernel,
        [((size, width), F32), ((width, width), F32), ((1, width), F32), ((1, width), F32)],
        rep, weights, others, sums[0], *away, scalar=True, far_out=(0, 1, 2, 3),
    )
    return embed, grad_embed, grad_dec1, grad_bias1[0], grad_dec2[0]


def solution(mesh):
    placed = (
        P("dom", None), P("dom", None), P("dom", None), P("dom", None), P("dom", None),
        P(), P(), P(),
        P(("dom", "rep"), None), P(("dom", "rep"), None), P(("dom", "rep")),
        P(), P(), P(),
    )
    return jax.shard_map(
        per_device,
        mesh=mesh,
        in_specs=placed,
        out_specs=(P("dom", None), P(("dom", "rep"), None), P(), P(), P()),
        check_vma=False,
    )
```

```python
import functools

import jax
import jax.numpy as jnp
from jax import lax
from jax.experimental import pallas as pl
from jax.experimental.pallas import tpu as pltpu
from jax.sharding import PartitionSpec as P

F32 = jnp.float32
BF16 = jnp.bfloat16
I32 = jnp.int32
VMEM_BYTES = 24 * 1024 * 1024
CHUNKS = 4
SPARE = 8
X_PARTS = 2


def iota(shape, dim):
    return lax.broadcasted_iota(I32, shape, dim)


def split_index(index, size):
    if size & (size - 1) == 0:
        return lax.shift_right_logical(index, size.bit_length() - 1), index & (size - 1)
    return lax.div(index, size), lax.rem(index, size)


def dot(a, b, dims=((1,), (0,))):
    return lax.dot_general(a, b, (dims, ((), ())), preferred_element_type=F32)


def exact_dot(a, ids, dims, ids_first):
    high = lax.shift_right_logical(ids, 8).astype(F32).astype(BF16)
    low = (ids & 255).astype(F32).astype(BF16)
    if ids_first:
        return dot(high, a, dims) * 256.0 + dot(low, a, dims)
    return dot(a, high, dims) * 256.0 + dot(a, low, dims)


def ones_where(mask):
    return jnp.where(mask, 1.0, 0.0).astype(BF16)


def as_column(ids, count):
    n, w = ids.shape
    rows = n * count
    source, _ = split_index(iota((rows, n), 0), count)
    picked = exact_dot(ones_where(source == iota((rows, n), 1)), ids, ((1,), (0,)), False)
    _, lane = split_index(iota((rows, w), 0), count)
    return jnp.sum(jnp.where(lane == iota((rows, w), 1), picked, 0.0), axis=1, keepdims=True).astype(I32)


def as_row(ids, count):
    n, w = ids.shape
    rows = n * count
    _, lane = split_index(iota((w, rows), 1), count)
    picked = exact_dot(ones_where(lane == iota((w, rows), 0)), ids, ((1,), (0,)), True)
    source, _ = split_index(iota((n, rows), 1), count)
    return jnp.sum(jnp.where(source == iota((n, rows), 0), picked, 0.0), axis=0, keepdims=True).astype(I32)


def row_to_column(row):
    size = row.shape[1]
    same = iota((size, size), 0) == iota((size, size), 1)
    return jnp.sum(jnp.where(same, row, 0.0), axis=1, keepdims=True)


def loads(sources, targets, sem):
    copies = [pltpu.make_async_copy(src, dst, sem.at[i]) for i, (src, dst) in enumerate(zip(sources, targets))]
    for copy in copies:
        copy.start()
    return copies


def wait(copies):
    for copy in copies:
        copy.wait()


def request_kernel(cap, joint, owner_hbm, local_hbm, halo_hbm, word_ref, place_ref, owner_ref, local_ref, halo_ref, sem):
    wait(loads((owner_hbm, local_hbm, halo_hbm), (owner_ref, local_ref, halo_ref), sem))
    n = word_ref.shape[0]
    owner = jnp.concatenate([owner_ref[0:1, :], owner_ref[1:2, :]], axis=1)
    local = jnp.concatenate([local_ref[0:1, :], local_ref[1:2, :]], axis=1)
    ends = owner.shape[1]
    match = iota((n, ends), 0) == owner
    upto = ones_where(iota((ends, ends), 0) <= iota((ends, ends), 1))
    count = dot(ones_where(match), upto)
    slot = jnp.sum(jnp.where(match, count, 0.0), axis=0, keepdims=True).astype(I32) - 1
    place_ref[...] = owner * cap + slot
    at_slot = ones_where(iota((cap, ends), 0) == slot)
    wanted = jnp.where(match, local, 0)
    ids = exact_dot(at_slot, wanted, ((1,), (1,)), True).astype(I32)
    word_ref[...] = ids
    if joint:
        halo = halo_ref.shape[1]
        word_ref[:, :halo] = ids[:, :halo] + lax.shift_left(halo_ref[...], 16)


def store(value, buffer, out_ref, sem, chunks):
    rows = out_ref.shape[0] // chunks
    copies = []
    for j in range(chunks):
        at = pl.ds(j * rows, rows)
        buffer[at, :] = value(j * rows, rows)
        copy = pltpu.make_async_copy(buffer.at[at, :], out_ref.at[at, :], sem.at[j])
        copy.start()
        copies.append(copy)
    return copies


def inner_kernel(
    feats_hbm, inner_hbm, self_hbm, b_hbm, halo_hbm, nbr_hbm, history_hbm,
    agg_ref, base_ref, halo_ref, nbr_ref, history_ref, feats_ref, inner_ref, self_ref, b_ref, sem,
):
    copies = loads(
        (feats_hbm, inner_hbm, self_hbm, b_hbm, halo_hbm, nbr_hbm, history_hbm),
        (feats_ref, inner_ref, self_ref, b_ref, halo_ref, nbr_ref, history_ref), sem,
    )
    wait(copies)
    feats = feats_ref[...]
    agg_ref[...] = dot(inner_ref[...], feats)
    base_ref[...] = dot(feats, self_ref[...]) + b_ref[...]


def edge_mask_kernel(
    place_ref, label_hbm, w1_hbm, b1_hbm, w2_hbm,
    gather_ref, scatter_ref, target_ref, w1_ref, b1_ref, w2_ref, label_ref, sem,
):
    copies = loads((label_hbm, w1_hbm, b1_hbm, w2_hbm), (label_ref, w1_ref, b1_ref, w2_ref), sem)
    place = place_ref[...]
    column = row_to_column(place.astype(F32)).astype(I32)
    gather_ref[...] = ones_where(column == iota(gather_ref.shape, 1))
    scatter_ref[...] = ones_where(iota(scatter_ref.shape, 0) == place)
    wait(copies)
    target_ref[...] = row_to_column(label_ref[...].astype(F32))


def sum_mask_kernel(cap, rep_ref, word_ref, *mask_refs):
    ids = as_row(word_ref[...] & 65535, cap)
    size = mask_refs[0].shape[0]
    for j, mask_ref in enumerate(mask_refs):
        node = iota((size, ids.shape[1]), 0) + (rep_ref[0] ^ j) * size
        mask_ref[...] = ones_where(node == ids)


def halo_kernel(cap, cap_edge, word_ref, history_ref, out_ref, ids_ref):
    ids_ref[...] = as_column(word_ref[...] & 65535, cap_edge)
    ids = as_column(lax.shift_right_logical(word_ref[...], 16), cap)
    nodes = history_ref.shape[0]
    out_ref[...] = dot(ones_where(ids == iota((ids.shape[0], nodes), 1)), history_ref[...]).astype(BF16)


def halo_and_ids_kernel(asked_ref, wanted_ref, history_ref, out_ref):
    n, cap = asked_ref.shape
    ids = as_column(asked_ref[...], cap)
    rows = dot(ones_where(ids == iota((n * cap, history_ref.shape[0]), 1)), history_ref[...])
    wanted = wanted_ref[...]
    spare, half = out_ref.shape[1] - cap, out_ref.shape[2] // 2
    blank = jnp.zeros((n, half - wanted.shape[1]), I32)
    parts = [lax.shift_right_logical(wanted, 8), blank, wanted & 255, blank]
    pairs = jnp.concatenate([part for part in parts if part.shape[1]], axis=1).astype(F32)
    for i in range(n):
        tail = jnp.broadcast_to(pairs[i:i + 1], (spare, 2 * half))
        out_ref[i] = jnp.concatenate([rows[i * cap:(i + 1) * cap], tail], axis=0).astype(BF16)


def embed_kernel(
    cap, agg_ref, base_ref, halo_ref, adj_ref, w_ref, ids_ref,
    embed_hbm, out_hbm, word_ref, embed_ref, out_ref, embed_sem, out_sem,
):
    if cap:
        n, rows, width = halo_ref.shape
        chunks = [halo_ref[i].astype(F32) for i in range(n)]
        halo = jnp.concatenate([chunk[:rows - SPARE] for chunk in chunks], axis=0).astype(BF16)
        pairs = jnp.concatenate([chunk[rows - SPARE:rows - SPARE + 1] for chunk in chunks], axis=0)
        half = width // 2
        word = (pairs[:, :cap] * 256.0 + pairs[:, half:half + cap]).astype(I32)
        word_ref[...] = word
        ids = as_column(word, cap)
    else:
        halo, ids = halo_ref[...], ids_ref[...]
        word_ref[...] = jnp.zeros(word_ref.shape, I32)
    agg = (agg_ref[...] + dot(adj_ref[...], halo)).astype(BF16)
    embed = jnp.maximum(base_ref[...] + dot(agg, w_ref[...]), 0.0).astype(BF16)
    copies = store(lambda at, size: embed[at:at + size], embed_ref, embed_hbm, embed_sem, 1)

    def fetched(at, size):
        return dot(ones_where(ids[at:at + size, :] == iota((size, embed.shape[0]), 1)), embed).astype(BF16)

    copies += store(fetched, out_ref, out_hbm, out_sem, CHUNKS)
    wait(copies)


def decode_kernel(
    rep_ref, ends_ref, gather_ref, scatter_ref, target_ref, w1_ref, b1_ref, w2_ref,
    grads_hbm, weights_ref, grads_ref, sem,
):
    rows = dot(gather_ref[...], ends_ref[...])
    queries = rows.shape[0] // 2
    head, tail = rows[:queries], rows[queries:]
    z = (head * tail).astype(BF16)
    w1 = w1_ref[...]
    pre = dot(z, w1) + b1_ref[...]
    sig = jax.nn.sigmoid(pre)
    hidden = (pre * sig).astype(BF16).astype(F32)
    w2 = w2_ref[...].astype(F32)
    logit = jnp.sum(hidden * w2, axis=1, keepdims=True)
    dlogit = jax.nn.sigmoid(logit) - target_ref[...]
    d_pre = (dlogit * w2 * (sig * (1.0 + pre * (1.0 - sig)))).astype(BF16)
    dz = dot(d_pre, w1, ((1,), (1,)))
    grads = jnp.concatenate([dz * tail, dz * head], axis=0).astype(BF16)
    copies = store(
        lambda at, size: dot(scatter_ref[at:at + size, :], grads).astype(BF16), grads_ref, grads_hbm, sem, CHUNKS
    )
    grad = dot(z, d_pre, ((0,), (0,)))
    half = grad.shape[0] // 2
    odd = (rep_ref[0] & 1) == 1
    low, high = grad[:half], grad[half:]
    bias = jnp.sum(d_pre.astype(F32), axis=0, keepdims=True)
    outer = jnp.sum(hidden * dlogit, axis=0, keepdims=True)
    first = iota((weights_ref.shape[0] // 2 - half, grad.shape[1]), 0)
    aux = jnp.where(first == 0, bias, jnp.where(first == 1, outer, 0.0))
    weights_ref[...] = jnp.concatenate([jnp.where(odd, high, low), aux, jnp.where(odd, low, high), aux], axis=0)
    wait(copies)


def final_kernel(rep_ref, mine_ref, other_ref, keep_ref, *refs):
    away_refs, (sums_ref, grad_ref, bias_ref, outer_ref) = refs[:-4], refs[-4:]
    rows = keep_ref.shape[0] // max(1, len(away_refs))
    for i, away_ref in enumerate(away_refs):
        at = pl.ds(i * rows, rows)
        sums_ref[at, :] = keep_ref[at, :] + away_ref[...].astype(F32)
    if not away_refs:
        sums_ref[...] = keep_ref[...]
    half = grad_ref.shape[0] // 2
    odd = (rep_ref[0] & 1) == 1
    mine, other = mine_ref[...], other_ref[...]
    low = jnp.where(odd, other, mine)
    grad_ref[:half] = low[:half]
    grad_ref[half:] = jnp.where(odd, mine, other)[:half]
    bias_ref[...] = low[half:half + 1]
    outer_ref[...] = low[half + 1:half + 2]


def scatter_kernel(mask_ref, grads_ref, out_ref):
    out_ref[...] = dot(mask_ref[...], grads_ref[...]).astype(out_ref.dtype)


def call(kernel, outs, *args, scalar=False, hbm_in=(), hbm_out=(), far_out=(), scratch=()):
    far_out = tuple(far_out) + tuple(hbm_out)
    space = pl.BlockSpec(memory_space=pltpu.VMEM)
    far = pl.BlockSpec(memory_space=pltpu.HBM)
    in_specs = [far if i in hbm_in else space for i in range(len(args))]
    if scalar:
        in_specs[0] = pl.BlockSpec(memory_space=pltpu.SMEM)
    args = [pltpu.with_memory_space_constraint(x, pltpu.HBM) if i in hbm_in else x for i, x in enumerate(args)]
    return pl.pallas_call(
        kernel,
        out_shape=[(pltpu.HBM if i in far_out else pltpu.VMEM)(s, t) for i, (s, t) in enumerate(outs)],
        in_specs=in_specs,
        out_specs=[far if i in hbm_out else space for i in range(len(outs))],
        scratch_shapes=list(scratch),
        compiler_params=pltpu.CompilerParams(vmem_limit_bytes=VMEM_BYTES),
    )(*args)


def swap(x, axis, mask):
    return lax.ppermute(x, axis, [(i, i ^ mask) for i in range(lax.axis_size(axis))])


def reduce_pairs(x, axis, mask):
    mine = x.astype(BF16)
    return mine.astype(F32) + swap(mine, axis, mask).astype(F32)


def reduce_fours(x, axis, mask):
    mine = x.astype(BF16)
    first, second, third = (swap(mine, axis, mask * k).astype(F32) for k in (1, 2, 3))
    return (mine.astype(F32) + first) + (second + third)


def exchange(x, axis):
    return lax.all_to_all(x, axis, split_axis=0, concat_axis=0, tiled=True)


def per_device(
    feats, history, adj_inner, adj_halo, halo_rows, w_self, w_nbr, b_enc,
    edge_owner, edge_rows, labels, w_dec1, b_dec1, w_dec2,
):
    n_dom = lax.axis_size("dom")
    n_rep = lax.axis_size("rep")
    nodes, width = feats.shape
    queries = edge_owner.shape[0]
    cap_halo = halo_rows.shape[1]
    cap = max(2, 4 * queries // n_dom)
    slots = n_dom * cap
    rep = lax.axis_index("rep").astype(I32).reshape(1)

    ends = 2 * queries
    ride = cap_halo % 16 == 0 and cap <= width // 2
    if ride:
        asked = exchange(halo_rows, "dom")
    word, place = call(
        functools.partial(request_kernel, cap, not ride),
        [((n_dom, cap), I32), ((1, ends), I32)],
        edge_owner.T, edge_rows.T, halo_rows,
        far_out=() if ride else (0,),
        hbm_in=(0, 1, 2),
        scratch=(
            pltpu.VMEM((2, queries), I32), pltpu.VMEM((2, queries), I32), pltpu.VMEM(halo_rows.shape, I32),
            pltpu.SemaphoreType.DMA((3,)),
        ),
    )
    if not ride:
        word = exchange(word, "dom")
    agg, base, adj_halo, w_nbr, history = call(
        inner_kernel,
        [
            ((nodes, width), F32), ((nodes, width), F32),
            (adj_halo.shape, BF16), (w_nbr.shape, BF16), (history.shape, BF16),
        ],
        feats, adj_inner, w_self, b_enc.reshape(1, -1), adj_halo, w_nbr, history,
        hbm_in=(0, 1, 2, 3, 4, 5, 6),
        scratch=(
            pltpu.VMEM(feats.shape, BF16), pltpu.VMEM(adj_inner.shape, BF16), pltpu.VMEM(w_self.shape, BF16),
            pltpu.VMEM((1, width), F32), pltpu.SemaphoreType.DMA((7,)),
        ),
    )
    if ride:
        (halo,) = call(
            halo_and_ids_kernel, [((n_dom, cap_halo + SPARE, width), BF16)], asked, word, history
        )
        halo = exchange(halo, "dom")
        ids = jnp.zeros((8, 128), I32)
    else:
        halo, ids = call(
            functools.partial(halo_kernel, cap_halo, cap),
            [((n_dom * cap_halo, width), BF16), ((slots, 1), I32)],
            word, history,
        )
        halo = exchange(halo.reshape(n_dom, cap_halo, width), "dom").reshape(-1, width)
    embed, fetched, got = call(
        functools.partial(embed_kernel, cap if ride else 0),
        [((nodes, width), BF16), ((slots, width), BF16), ((n_dom, cap), I32)],
        agg, base, halo, adj_halo, w_nbr, ids,
        hbm_out=(0, 1),
        scratch=(
            pltpu.VMEM((nodes, width), BF16), pltpu.VMEM((slots, width), BF16),
            pltpu.SemaphoreType.DMA((1,)), pltpu.SemaphoreType.DMA((CHUNKS,)),
        ),
    )
    word = got if ride else word
    fetched = exchange(fetched.reshape(n_dom, cap, width), "dom").reshape(-1, width)
    gather, scatter, target, w1, b1, w2 = call(
        edge_mask_kernel,
        [
            ((ends, slots), BF16), ((slots, ends), BF16), ((queries, 1), F32),
            (w_dec1.shape, BF16), ((1, width), F32), ((1, width), BF16),
        ],
        place, labels.reshape(1, -1), w_dec1, b_dec1.reshape(1, -1), w_dec2.reshape(1, -1),
        hbm_in=(1, 2, 3, 4),
        scratch=(pltpu.VMEM((1, queries), I32), pltpu.SemaphoreType.DMA((4,))),
    )
    half = width // 2
    placed, weights = call(
        decode_kernel,
        [((slots, width), BF16), ((2 * (half + 8), width), F32)],
        rep, fetched, gather, scatter, target, w1, b1, w2,
        scalar=True,
        hbm_out=(0,),
        scratch=(pltpu.VMEM((slots, width), BF16), pltpu.SemaphoreType.DMA((CHUNKS,))),
    )
    back = exchange(placed.reshape(n_dom, cap, width), "dom").reshape(-1, width)
    step = 2
    while step < n_rep:
        weights = reduce_pairs(weights, "rep", step)
        step *= 2
    keep, send = jnp.split(weights, 2, axis=0)
    weights = keep + swap(send, "rep", 1)
    step = 1
    while 4 * step <= n_dom // 2:
        weights = reduce_fours(weights, "dom", step)
        step *= 4

    back, weights = lax.optimization_barrier((back, weights))
    size = nodes // n_rep
    masks = call(
        functools.partial(sum_mask_kernel, cap), [((size, slots), BF16)] * n_rep, rep, word, scalar=True
    )

    def block_sum(j, dtype):
        (out,) = call(scatter_kernel, [((size, width), dtype)], masks[j], back)
        return out

    sums = {}
    for j in reversed(range(0, n_rep, 2)):
        send = block_sum(j + 1, BF16)
        sums[j] = block_sum(j, F32) + swap(send, "rep", 1).astype(F32)
    rep_step, away = 2, []
    while rep_step < n_rep:
        for j in range(0, n_rep, 2 * rep_step):
            parts = jnp.split(sums[j + rep_step].astype(BF16), X_PARTS, axis=0)
            away = [swap(part, "rep", rep_step) for part in parts]
            if step < n_dom:
                mine = weights.astype(BF16)
                others = swap(mine, "dom", step)
                others, away[0] = lax.optimization_barrier((others, away[0]))
                weights = mine.astype(F32) + others.astype(F32)
                step *= 2
            if 2 * rep_step < n_rep:
                sums[j] = sums[j] + jnp.concatenate(away, axis=0).astype(F32)
        rep_step *= 2
    while step < n_dom:
        weights = reduce_pairs(weights, "dom", step)
        step *= 2

    others = swap(weights, "rep", 1)
    grad_embed, grad_dec1, grad_bias1, grad_dec2 = call(
        final_kernel,
        [((size, width), F32), ((width, width), F32), ((1, width), F32), ((1, width), F32)],
        rep, weights, others, sums[0], *away, scalar=True, far_out=(0, 1, 2, 3),
    )
    return embed, grad_embed, grad_dec1, grad_bias1[0], grad_dec2[0]


def solution(mesh):
    placed = (
        P("dom", None), P("dom", None), P("dom", None), P("dom", None), P("dom", None),
        P(), P(), P(),
        P(("dom", "rep"), None), P(("dom", "rep"), None), P(("dom", "rep")),
        P(), P(), P(),
    )
    return jax.shard_map(
        per_device,
        mesh=mesh,
        in_specs=placed,
        out_specs=(P("dom", None), P(("dom", "rep"), None), P(), P(), P()),
        check_vma=False,
    )
```

```python
import functools

import jax
import jax.numpy as jnp
from jax import lax
from jax.experimental import pallas as pl
from jax.experimental.pallas import tpu as pltpu
from jax.sharding import PartitionSpec as P

F32 = jnp.float32
BF16 = jnp.bfloat16
I32 = jnp.int32
VMEM_BYTES = 24 * 1024 * 1024
CHUNKS = 4
SPARE = 8
X_PARTS = 2


def iota(shape, dim):
    return lax.broadcasted_iota(I32, shape, dim)


def split_index(index, size):
    if size & (size - 1) == 0:
        return lax.shift_right_logical(index, size.bit_length() - 1), index & (size - 1)
    return lax.div(index, size), lax.rem(index, size)


def dot(a, b, dims=((1,), (0,))):
    return lax.dot_general(a, b, (dims, ((), ())), preferred_element_type=F32)


def exact_dot(a, ids, dims, ids_first):
    high = lax.shift_right_logical(ids, 8).astype(F32).astype(BF16)
    low = (ids & 255).astype(F32).astype(BF16)
    if ids_first:
        return dot(high, a, dims) * 256.0 + dot(low, a, dims)
    return dot(a, high, dims) * 256.0 + dot(a, low, dims)


def ones_where(mask):
    return jnp.where(mask, 1.0, 0.0).astype(BF16)


def as_column(ids, count):
    n, w = ids.shape
    rows = n * count
    source, _ = split_index(iota((rows, n), 0), count)
    picked = exact_dot(ones_where(source == iota((rows, n), 1)), ids, ((1,), (0,)), False)
    _, lane = split_index(iota((rows, w), 0), count)
    return jnp.sum(jnp.where(lane == iota((rows, w), 1), picked, 0.0), axis=1, keepdims=True).astype(I32)


def as_row(ids, count):
    n, w = ids.shape
    rows = n * count
    _, lane = split_index(iota((w, rows), 1), count)
    picked = exact_dot(ones_where(lane == iota((w, rows), 0)), ids, ((1,), (0,)), True)
    source, _ = split_index(iota((n, rows), 1), count)
    return jnp.sum(jnp.where(source == iota((n, rows), 0), picked, 0.0), axis=0, keepdims=True).astype(I32)


def row_to_column(row):
    size = row.shape[1]
    same = iota((size, size), 0) == iota((size, size), 1)
    return jnp.sum(jnp.where(same, row, 0.0), axis=1, keepdims=True)


def loads(sources, targets, sem):
    copies = [pltpu.make_async_copy(src, dst, sem.at[i]) for i, (src, dst) in enumerate(zip(sources, targets))]
    for copy in copies:
        copy.start()
    return copies


def wait(copies):
    for copy in copies:
        copy.wait()


def request_kernel(cap, joint, owner_hbm, local_hbm, halo_hbm, word_ref, place_ref, owner_ref, local_ref, halo_ref, sem):
    wait(loads((owner_hbm, local_hbm, halo_hbm), (owner_ref, local_ref, halo_ref), sem))
    n = word_ref.shape[0]
    owner = jnp.concatenate([owner_ref[0:1, :], owner_ref[1:2, :]], axis=1)
    local = jnp.concatenate([local_ref[0:1, :], local_ref[1:2, :]], axis=1)
    ends = owner.shape[1]
    match = iota((n, ends), 0) == owner
    upto = ones_where(iota((ends, ends), 0) <= iota((ends, ends), 1))
    count = dot(ones_where(match), upto)
    slot = jnp.sum(jnp.where(match, count, 0.0), axis=0, keepdims=True).astype(I32) - 1
    place_ref[...] = owner * cap + slot
    at_slot = ones_where(iota((cap, ends), 0) == slot)
    wanted = jnp.where(match, local, 0)
    ids = exact_dot(at_slot, wanted, ((1,), (1,)), True).astype(I32)
    word_ref[...] = ids
    if joint:
        halo = halo_ref.shape[1]
        word_ref[:, :halo] = ids[:, :halo] + lax.shift_left(halo_ref[...], 16)


def store(value, buffer, out_ref, sem, chunks):
    rows = out_ref.shape[0] // chunks
    copies = []
    for j in range(chunks):
        at = pl.ds(j * rows, rows)
        buffer[at, :] = value(j * rows, rows)
        copy = pltpu.make_async_copy(buffer.at[at, :], out_ref.at[at, :], sem.at[j])
        copy.start()
        copies.append(copy)
    return copies


def inner_kernel(
    feats_hbm, inner_hbm, self_hbm, b_hbm, halo_hbm, nbr_hbm, history_hbm,
    agg_ref, base_ref, halo_ref, nbr_ref, history_ref, feats_ref, inner_ref, self_ref, b_ref, sem,
):
    copies = loads(
        (feats_hbm, inner_hbm, self_hbm, b_hbm, halo_hbm, nbr_hbm, history_hbm),
        (feats_ref, inner_ref, self_ref, b_ref, halo_ref, nbr_ref, history_ref), sem,
    )
    wait(copies)
    feats = feats_ref[...]
    agg_ref[...] = dot(inner_ref[...], feats)
    base_ref[...] = dot(feats, self_ref[...]) + b_ref[...]


def edge_mask_kernel(
    place_ref, label_hbm, w1_hbm, b1_hbm, w2_hbm,
    gather_ref, scatter_ref, target_ref, w1_ref, b1_ref, w2_ref, label_ref, sem,
):
    copies = loads((label_hbm, w1_hbm, b1_hbm, w2_hbm), (label_ref, w1_ref, b1_ref, w2_ref), sem)
    place = place_ref[...]
    column = row_to_column(place.astype(F32)).astype(I32)
    gather_ref[...] = ones_where(column == iota(gather_ref.shape, 1))
    scatter_ref[...] = ones_where(iota(scatter_ref.shape, 0) == place)
    wait(copies)
    target_ref[...] = row_to_column(label_ref[...].astype(F32))


def sum_mask_kernel(cap, rep_ref, word_ref, *mask_refs):
    ids = as_row(word_ref[...] & 65535, cap)
    size = mask_refs[0].shape[0]
    for j, mask_ref in enumerate(mask_refs):
        node = iota((size, ids.shape[1]), 0) + (rep_ref[0] ^ j) * size
        mask_ref[...] = ones_where(node == ids)


def halo_kernel(cap, cap_edge, word_ref, history_ref, out_ref, ids_ref):
    ids_ref[...] = as_column(word_ref[...] & 65535, cap_edge)
    ids = as_column(lax.shift_right_logical(word_ref[...], 16), cap)
    nodes = history_ref.shape[0]
    out_ref[...] = dot(ones_where(ids == iota((ids.shape[0], nodes), 1)), history_ref[...]).astype(BF16)


def halo_and_ids_kernel(asked_ref, wanted_ref, history_ref, out_ref):
    n, cap = asked_ref.shape
    ids = as_column(asked_ref[...], cap)
    rows = dot(ones_where(ids == iota((n * cap, history_ref.shape[0]), 1)), history_ref[...])
    wanted = wanted_ref[...]
    spare, half = out_ref.shape[1] - cap, out_ref.shape[2] // 2
    blank = jnp.zeros((n, half - wanted.shape[1]), I32)
    parts = [lax.shift_right_logical(wanted, 8), blank, wanted & 255, blank]
    pairs = jnp.concatenate([part for part in parts if part.shape[1]], axis=1).astype(F32)
    for i in range(n):
        tail = jnp.broadcast_to(pairs[i:i + 1], (spare, 2 * half))
        out_ref[i] = jnp.concatenate([rows[i * cap:(i + 1) * cap], tail], axis=0).astype(BF16)


def embed_kernel(
    cap, agg_ref, base_ref, halo_ref, adj_ref, w_ref, ids_ref,
    embed_hbm, out_hbm, word_ref, embed_ref, out_ref, embed_sem, out_sem,
):
    if cap:
        n, rows, width = halo_ref.shape
        chunks = [halo_ref[i].astype(F32) for i in range(n)]
        halo = jnp.concatenate([chunk[:rows - SPARE] for chunk in chunks], axis=0).astype(BF16)
        pairs = jnp.concatenate([chunk[rows - SPARE:rows - SPARE + 1] for chunk in chunks], axis=0)
        half = width // 2
        word = (pairs[:, :cap] * 256.0 + pairs[:, half:half + cap]).astype(I32)
        word_ref[...] = word
        ids = as_column(word, cap)
    else:
        halo, ids = halo_ref[...], ids_ref[...]
        word_ref[...] = jnp.zeros(word_ref.shape, I32)
    agg = (agg_ref[...] + dot(adj_ref[...], halo)).astype(BF16)
    embed = jnp.maximum(base_ref[...] + dot(agg, w_ref[...]), 0.0).astype(BF16)
    copies = store(lambda at, size: embed[at:at + size], embed_ref, embed_hbm, embed_sem, 1)

    def fetched(at, size):
        return dot(ones_where(ids[at:at + size, :] == iota((size, embed.shape[0]), 1)), embed).astype(BF16)

    copies += store(fetched, out_ref, out_hbm, out_sem, CHUNKS)
    wait(copies)


def decode_kernel(
    rep_ref, ends_ref, gather_ref, scatter_ref, target_ref, w1_ref, b1_ref, w2_ref,
    grads_hbm, weights_ref, grads_ref, sem,
):
    rows = dot(gather_ref[...], ends_ref[...])
    queries = rows.shape[0] // 2
    head, tail = rows[:queries], rows[queries:]
    z = (head * tail).astype(BF16)
    w1 = w1_ref[...]
    pre = dot(z, w1) + b1_ref[...]
    sig = jax.nn.sigmoid(pre)
    hidden = (pre * sig).astype(BF16).astype(F32)
    w2 = w2_ref[...].astype(F32)
    logit = jnp.sum(hidden * w2, axis=1, keepdims=True)
    dlogit = jax.nn.sigmoid(logit) - target_ref[...]
    d_pre = (dlogit * w2 * (sig * (1.0 + pre * (1.0 - sig)))).astype(BF16)
    dz = dot(d_pre, w1, ((1,), (1,)))
    grads = jnp.concatenate([dz * tail, dz * head], axis=0).astype(BF16)
    copies = store(
        lambda at, size: dot(scatter_ref[at:at + size, :], grads).astype(BF16), grads_ref, grads_hbm, sem, CHUNKS
    )
    grad = dot(z, d_pre, ((0,), (0,)))
    half = grad.shape[0] // 2
    odd = (rep_ref[0] & 1) == 1
    low, high = grad[:half], grad[half:]
    bias = jnp.sum(d_pre.astype(F32), axis=0, keepdims=True)
    outer = jnp.sum(hidden * dlogit, axis=0, keepdims=True)
    first = iota((weights_ref.shape[0] // 2 - half, grad.shape[1]), 0)
    aux = jnp.where(first == 0, bias, jnp.where(first == 1, outer, 0.0))
    weights_ref[...] = jnp.concatenate([jnp.where(odd, high, low), aux, jnp.where(odd, low, high), aux], axis=0)
    wait(copies)


def final_kernel(rep_ref, mine_ref, other_ref, keep_ref, *refs):
    away_refs, (sums_ref, grad_ref, bias_ref, outer_ref) = refs[:-4], refs[-4:]
    rows = keep_ref.shape[0] // max(1, len(away_refs))
    for i, away_ref in enumerate(away_refs):
        at = pl.ds(i * rows, rows)
        sums_ref[at, :] = keep_ref[at, :] + away_ref[...].astype(F32)
    if not away_refs:
        sums_ref[...] = keep_ref[...]
    half = grad_ref.shape[0] // 2
    odd = (rep_ref[0] & 1) == 1
    mine, other = mine_ref[...], other_ref[...]
    low = jnp.where(odd, other, mine)
    grad_ref[:half] = low[:half]
    grad_ref[half:] = jnp.where(odd, mine, other)[:half]
    bias_ref[...] = low[half:half + 1]
    outer_ref[...] = low[half + 1:half + 2]


def scatter_kernel(grads_ref, *refs):
    count = len(refs) // 2
    for mask_ref, out_ref in zip(refs[:count], refs[count:]):
        out_ref[...] = dot(mask_ref[...], grads_ref[...]).astype(out_ref.dtype)


def call(kernel, outs, *args, scalar=False, hbm_in=(), hbm_out=(), far_out=(), scratch=()):
    far_out = tuple(far_out) + tuple(hbm_out)
    space = pl.BlockSpec(memory_space=pltpu.VMEM)
    far = pl.BlockSpec(memory_space=pltpu.HBM)
    in_specs = [far if i in hbm_in else space for i in range(len(args))]
    if scalar:
        in_specs[0] = pl.BlockSpec(memory_space=pltpu.SMEM)
    args = [pltpu.with_memory_space_constraint(x, pltpu.HBM) if i in hbm_in else x for i, x in enumerate(args)]
    return pl.pallas_call(
        kernel,
        out_shape=[(pltpu.HBM if i in far_out else pltpu.VMEM)(s, t) for i, (s, t) in enumerate(outs)],
        in_specs=in_specs,
        out_specs=[far if i in hbm_out else space for i in range(len(outs))],
        scratch_shapes=list(scratch),
        compiler_params=pltpu.CompilerParams(vmem_limit_bytes=VMEM_BYTES),
    )(*args)


def swap(x, axis, mask):
    return lax.ppermute(x, axis, [(i, i ^ mask) for i in range(lax.axis_size(axis))])


def rounded(x):
    return lax.reduce_precision(x, exponent_bits=8, mantissa_bits=7)


def reduce_pairs(x, axis, mask):
    mine = rounded(x)
    return mine + swap(mine.astype(BF16), axis, mask).astype(F32)


def reduce_fours(x, axis, mask):
    mine = rounded(x)
    first, second, third = (swap(mine.astype(BF16), axis, mask * k).astype(F32) for k in (1, 2, 3))
    return (mine + first) + (second + third)


def exchange(x, axis):
    return lax.all_to_all(x, axis, split_axis=0, concat_axis=0, tiled=True)


def per_device(
    feats, history, adj_inner, adj_halo, halo_rows, w_self, w_nbr, b_enc,
    edge_owner, edge_rows, labels, w_dec1, b_dec1, w_dec2,
):
    n_dom = lax.axis_size("dom")
    n_rep = lax.axis_size("rep")
    nodes, width = feats.shape
    queries = edge_owner.shape[0]
    cap_halo = halo_rows.shape[1]
    cap = max(2, 4 * queries // n_dom)
    slots = n_dom * cap
    rep = lax.axis_index("rep").astype(I32).reshape(1)

    ends = 2 * queries
    ride = cap_halo % 16 == 0 and cap <= width // 2
    if ride:
        asked = exchange(halo_rows, "dom")
    word, place = call(
        functools.partial(request_kernel, cap, not ride),
        [((n_dom, cap), I32), ((1, ends), I32)],
        edge_owner.T, edge_rows.T, halo_rows,
        far_out=() if ride else (0,),
        hbm_in=(0, 1, 2),
        scratch=(
            pltpu.VMEM((2, queries), I32), pltpu.VMEM((2, queries), I32), pltpu.VMEM(halo_rows.shape, I32),
            pltpu.SemaphoreType.DMA((3,)),
        ),
    )
    if not ride:
        word = exchange(word, "dom")
    agg, base, adj_halo, w_nbr, history = call(
        inner_kernel,
        [
            ((nodes, width), F32), ((nodes, width), F32),
            (adj_halo.shape, BF16), (w_nbr.shape, BF16), (history.shape, BF16),
        ],
        feats, adj_inner, w_self, b_enc.reshape(1, -1), adj_halo, w_nbr, history,
        hbm_in=(0, 1, 2, 3, 4, 5, 6),
        scratch=(
            pltpu.VMEM(feats.shape, BF16), pltpu.VMEM(adj_inner.shape, BF16), pltpu.VMEM(w_self.shape, BF16),
            pltpu.VMEM((1, width), F32), pltpu.SemaphoreType.DMA((7,)),
        ),
    )
    if ride:
        (halo,) = call(
            halo_and_ids_kernel, [((n_dom, cap_halo + SPARE, width), BF16)], asked, word, history
        )
        halo = exchange(halo, "dom")
        ids = jnp.zeros((8, 128), I32)
    else:
        halo, ids = call(
            functools.partial(halo_kernel, cap_halo, cap),
            [((n_dom * cap_halo, width), BF16), ((slots, 1), I32)],
            word, history,
        )
        halo = exchange(halo.reshape(n_dom, cap_halo, width), "dom").reshape(-1, width)
    embed, fetched, got = call(
        functools.partial(embed_kernel, cap if ride else 0),
        [((nodes, width), BF16), ((slots, width), BF16), ((n_dom, cap), I32)],
        agg, base, halo, adj_halo, w_nbr, ids,
        hbm_out=(0, 1),
        scratch=(
            pltpu.VMEM((nodes, width), BF16), pltpu.VMEM((slots, width), BF16),
            pltpu.SemaphoreType.DMA((1,)), pltpu.SemaphoreType.DMA((CHUNKS,)),
        ),
    )
    word = got if ride else word
    fetched = exchange(fetched.reshape(n_dom, cap, width), "dom").reshape(-1, width)
    gather, scatter, target, w1, b1, w2 = call(
        edge_mask_kernel,
        [
            ((ends, slots), BF16), ((slots, ends), BF16), ((queries, 1), F32),
            (w_dec1.shape, BF16), ((1, width), F32), ((1, width), BF16),
        ],
        place, labels.reshape(1, -1), w_dec1, b_dec1.reshape(1, -1), w_dec2.reshape(1, -1),
        hbm_in=(1, 2, 3, 4),
        scratch=(pltpu.VMEM((1, queries), I32), pltpu.SemaphoreType.DMA((4,))),
    )
    half = width // 2
    placed, weights = call(
        decode_kernel,
        [((slots, width), BF16), ((2 * (half + 16), width), F32)],
        rep, fetched, gather, scatter, target, w1, b1, w2,
        scalar=True,
        hbm_out=(0,),
        scratch=(pltpu.VMEM((slots, width), BF16), pltpu.SemaphoreType.DMA((CHUNKS,))),
    )
    back = exchange(placed.reshape(n_dom, cap, width), "dom").reshape(-1, width)
    keep, send = jnp.split(rounded(weights), 2, axis=0)
    weights = keep + swap(send.astype(BF16), "rep", 1).astype(F32)
    if n_rep > 2:
        second, third = swap(keep.astype(BF16), "rep", 2), swap(send.astype(BF16), "rep", 3)
        weights = weights + (second.astype(F32) + third.astype(F32))
    step = 4
    while step < n_rep:
        weights = reduce_pairs(weights, "rep", step)
        step *= 2
    step = 1
    while 4 * step <= n_dom // 2:
        mine = rounded(weights)
        parts = [swap(mine.astype(BF16), "dom", step * k) for k in (1, 2, 3)]
        back, *parts[:2] = lax.optimization_barrier((back, *parts[:2]))
        first, second, third = (part.astype(F32) for part in parts)
        weights = (mine + first) + (second + third)
        step *= 4
    size = nodes // n_rep
    masks = call(
        functools.partial(sum_mask_kernel, cap), [((size, slots), BF16)] * n_rep, rep, word, scalar=True
    )

    block = {}
    for group in (range(n_rep - 1, 0, -2), range(n_rep - 2, -1, -2)):
        outs = call(
            scatter_kernel,
            [((size, width), BF16 if j % 2 else F32) for j in group],
            back, *(masks[j] for j in group),
        )
        block.update(zip(group, outs))
    sums = {j: block[j] + swap(block[j + 1], "rep", 1).astype(F32) for j in reversed(range(0, n_rep, 2))}
    rep_step, away = 2, []
    while rep_step < n_rep:
        for j in range(0, n_rep, 2 * rep_step):
            parts = jnp.split(sums[j + rep_step].astype(BF16), X_PARTS, axis=0)
            away = [swap(part, "rep", rep_step) for part in parts]
            if step < n_dom:
                mine = rounded(weights)
                others = swap(mine.astype(BF16), "dom", step)
                others, away[0] = lax.optimization_barrier((others, away[0]))
                weights = mine + others.astype(F32)
                step *= 2
            if 2 * rep_step < n_rep:
                sums[j] = sums[j] + jnp.concatenate(away, axis=0).astype(F32)
        rep_step *= 2
    while step < n_dom:
        weights = reduce_pairs(weights, "dom", step)
        step *= 2

    others = swap(weights, "rep", 1)
    grad_embed, grad_dec1, grad_bias1, grad_dec2 = call(
        final_kernel,
        [((size, width), F32), ((width, width), F32), ((1, width), F32), ((1, width), F32)],
        rep, weights, others, sums[0], *away, scalar=True, far_out=(0, 1, 2, 3),
    )
    return embed, grad_embed, grad_dec1, grad_bias1[0], grad_dec2[0]


def solution(mesh):
    placed = (
        P("dom", None), P("dom", None), P("dom", None), P("dom", None), P("dom", None),
        P(), P(), P(),
        P(("dom", "rep"), None), P(("dom", "rep"), None), P(("dom", "rep")),
        P(), P(), P(),
    )
    return jax.shard_map(
        per_device,
        mesh=mesh,
        in_specs=placed,
        out_specs=(P("dom", None), P(("dom", "rep"), None), P(), P(), P()),
        check_vma=False,
    )
```

```python
import functools

import jax
import jax.numpy as jnp
from jax import lax
from jax.experimental import pallas as pl
from jax.experimental.pallas import tpu as pltpu
from jax.sharding import PartitionSpec as P

F32 = jnp.float32
BF16 = jnp.bfloat16
I32 = jnp.int32
VMEM_BYTES = 24 * 1024 * 1024
CHUNKS = 4
SPARE = 8
X_PARTS = 2


def iota(shape, dim):
    return lax.broadcasted_iota(I32, shape, dim)


def split_index(index, size):
    if size & (size - 1) == 0:
        return lax.shift_right_logical(index, size.bit_length() - 1), index & (size - 1)
    return lax.div(index, size), lax.rem(index, size)


def dot(a, b, dims=((1,), (0,))):
    return lax.dot_general(a, b, (dims, ((), ())), preferred_element_type=F32)


def exact_dot(a, ids, dims, ids_first):
    high = lax.shift_right_logical(ids, 8).astype(F32).astype(BF16)
    low = (ids & 255).astype(F32).astype(BF16)
    if ids_first:
        return dot(high, a, dims) * 256.0 + dot(low, a, dims)
    return dot(a, high, dims) * 256.0 + dot(a, low, dims)


def ones_where(mask):
    return jnp.where(mask, 1.0, 0.0).astype(BF16)


def as_column(ids, count):
    n, w = ids.shape
    rows = n * count
    source, _ = split_index(iota((rows, n), 0), count)
    picked = exact_dot(ones_where(source == iota((rows, n), 1)), ids, ((1,), (0,)), False)
    _, lane = split_index(iota((rows, w), 0), count)
    return jnp.sum(jnp.where(lane == iota((rows, w), 1), picked, 0.0), axis=1, keepdims=True).astype(I32)


def as_row(ids, count):
    n, w = ids.shape
    rows = n * count
    _, lane = split_index(iota((w, rows), 1), count)
    picked = exact_dot(ones_where(lane == iota((w, rows), 0)), ids, ((1,), (0,)), True)
    source, _ = split_index(iota((n, rows), 1), count)
    return jnp.sum(jnp.where(source == iota((n, rows), 0), picked, 0.0), axis=0, keepdims=True).astype(I32)


def row_to_column(row):
    size = row.shape[1]
    same = iota((size, size), 0) == iota((size, size), 1)
    return jnp.sum(jnp.where(same, row, 0.0), axis=1, keepdims=True)


def loads(sources, targets, sem):
    copies = [pltpu.make_async_copy(src, dst, sem.at[i]) for i, (src, dst) in enumerate(zip(sources, targets))]
    for copy in copies:
        copy.start()
    return copies


def wait(copies):
    for copy in copies:
        copy.wait()


def request_kernel(cap, joint, owner_hbm, local_hbm, halo_hbm, word_ref, place_ref, owner_ref, local_ref, halo_ref, sem):
    wait(loads((owner_hbm, local_hbm, halo_hbm), (owner_ref, local_ref, halo_ref), sem))
    n = word_ref.shape[0]
    owner = jnp.concatenate([owner_ref[0:1, :], owner_ref[1:2, :]], axis=1)
    local = jnp.concatenate([local_ref[0:1, :], local_ref[1:2, :]], axis=1)
    ends = owner.shape[1]
    match = iota((n, ends), 0) == owner
    upto = ones_where(iota((ends, ends), 0) <= iota((ends, ends), 1))
    count = dot(ones_where(match), upto)
    slot = jnp.sum(jnp.where(match, count, 0.0), axis=0, keepdims=True).astype(I32) - 1
    place_ref[...] = owner * cap + slot
    at_slot = ones_where(iota((cap, ends), 0) == slot)
    wanted = jnp.where(match, local, 0)
    ids = exact_dot(at_slot, wanted, ((1,), (1,)), True).astype(I32)
    word_ref[...] = ids
    if joint:
        halo = halo_ref.shape[1]
        word_ref[:, :halo] = ids[:, :halo] + lax.shift_left(halo_ref[...], 16)


def store(value, buffer, out_ref, sem, chunks):
    rows = out_ref.shape[0] // chunks
    copies = []
    for j in range(chunks):
        at = pl.ds(j * rows, rows)
        buffer[at, :] = value(j * rows, rows)
        copy = pltpu.make_async_copy(buffer.at[at, :], out_ref.at[at, :], sem.at[j])
        copy.start()
        copies.append(copy)
    return copies


def inner_kernel(
    feats_hbm, inner_hbm, self_hbm, b_hbm, halo_hbm, nbr_hbm, history_hbm,
    agg_ref, base_ref, halo_ref, nbr_ref, history_ref, feats_ref, inner_ref, self_ref, b_ref, sem,
):
    copies = loads(
        (feats_hbm, inner_hbm, self_hbm, b_hbm, halo_hbm, nbr_hbm, history_hbm),
        (feats_ref, inner_ref, self_ref, b_ref, halo_ref, nbr_ref, history_ref), sem,
    )
    wait(copies)
    feats = feats_ref[...]
    agg_ref[...] = dot(inner_ref[...], feats)
    base_ref[...] = dot(feats, self_ref[...]) + b_ref[...]


def edge_mask_kernel(
    place_ref, label_hbm, w1_hbm, b1_hbm, w2_hbm,
    gather_ref, scatter_ref, target_ref, w1_ref, b1_ref, w2_ref, label_ref, sem,
):
    copies = loads((label_hbm, w1_hbm, b1_hbm, w2_hbm), (label_ref, w1_ref, b1_ref, w2_ref), sem)
    place = place_ref[...]
    column = row_to_column(place.astype(F32)).astype(I32)
    gather_ref[...] = ones_where(column == iota(gather_ref.shape, 1))
    scatter_ref[...] = ones_where(iota(scatter_ref.shape, 0) == place)
    wait(copies)
    target_ref[...] = row_to_column(label_ref[...].astype(F32))


def sum_mask_kernel(cap, rep_ref, word_ref, *mask_refs):
    ids = as_row(word_ref[...] & 65535, cap)
    size = mask_refs[0].shape[0]
    for j, mask_ref in enumerate(mask_refs):
        node = iota((size, ids.shape[1]), 0) + (rep_ref[0] ^ j) * size
        mask_ref[...] = ones_where(node == ids)


def halo_kernel(cap, cap_edge, word_ref, history_ref, out_ref, ids_ref):
    ids_ref[...] = as_column(word_ref[...] & 65535, cap_edge)
    ids = as_column(lax.shift_right_logical(word_ref[...], 16), cap)
    nodes = history_ref.shape[0]
    out_ref[...] = dot(ones_where(ids == iota((ids.shape[0], nodes), 1)), history_ref[...]).astype(BF16)


def halo_and_ids_kernel(asked_ref, wanted_ref, history_ref, out_ref):
    n, cap = asked_ref.shape
    ids = as_column(asked_ref[...], cap)
    rows = dot(ones_where(ids == iota((n * cap, history_ref.shape[0]), 1)), history_ref[...])
    wanted = wanted_ref[...]
    spare, half = out_ref.shape[1] - cap, out_ref.shape[2] // 2
    blank = jnp.zeros((n, half - wanted.shape[1]), I32)
    parts = [lax.shift_right_logical(wanted, 8), blank, wanted & 255, blank]
    pairs = jnp.concatenate([part for part in parts if part.shape[1]], axis=1).astype(F32)
    for i in range(n):
        tail = jnp.broadcast_to(pairs[i:i + 1], (spare, 2 * half))
        out_ref[i] = jnp.concatenate([rows[i * cap:(i + 1) * cap], tail], axis=0).astype(BF16)


def embed_kernel(
    cap, agg_ref, base_ref, halo_ref, adj_ref, w_ref, ids_ref,
    embed_hbm, out_hbm, word_ref, embed_ref, out_ref, embed_sem, out_sem,
):
    if cap:
        n, rows, width = halo_ref.shape
        chunks = [halo_ref[i].astype(F32) for i in range(n)]
        halo = jnp.concatenate([chunk[:rows - SPARE] for chunk in chunks], axis=0).astype(BF16)
        pairs = jnp.concatenate([chunk[rows - SPARE:rows - SPARE + 1] for chunk in chunks], axis=0)
        half = width // 2
        word = (pairs[:, :cap] * 256.0 + pairs[:, half:half + cap]).astype(I32)
        word_ref[...] = word
        ids = as_column(word, cap)
    else:
        halo, ids = halo_ref[...], ids_ref[...]
        word_ref[...] = jnp.zeros(word_ref.shape, I32)
    agg = (agg_ref[...] + dot(adj_ref[...], halo)).astype(BF16)
    embed = jnp.maximum(base_ref[...] + dot(agg, w_ref[...]), 0.0).astype(BF16)
    copies = store(lambda at, size: embed[at:at + size], embed_ref, embed_hbm, embed_sem, 1)

    def fetched(at, size):
        return dot(ones_where(ids[at:at + size, :] == iota((size, embed.shape[0]), 1)), embed).astype(BF16)

    copies += store(fetched, out_ref, out_hbm, out_sem, CHUNKS)
    wait(copies)


def decode_kernel(
    rep_ref, ends_ref, gather_ref, scatter_ref, target_ref, w1_ref, b1_ref, w2_ref,
    grads_hbm, weights_ref, grads_ref, sem,
):
    rows = dot(gather_ref[...], ends_ref[...])
    queries = rows.shape[0] // 2
    head, tail = rows[:queries], rows[queries:]
    z = (head * tail).astype(BF16)
    w1 = w1_ref[...]
    pre = dot(z, w1) + b1_ref[...]
    sig = jax.nn.sigmoid(pre)
    hidden = (pre * sig).astype(BF16).astype(F32)
    w2 = w2_ref[...].astype(F32)
    logit = jnp.sum(hidden * w2, axis=1, keepdims=True)
    dlogit = jax.nn.sigmoid(logit) - target_ref[...]
    d_pre = (dlogit * w2 * (sig * (1.0 + pre * (1.0 - sig)))).astype(BF16)
    dz = dot(d_pre, w1, ((1,), (1,)))
    grads = jnp.concatenate([dz * tail, dz * head], axis=0).astype(BF16)
    copies = store(
        lambda at, size: dot(scatter_ref[at:at + size, :], grads).astype(BF16), grads_ref, grads_hbm, sem, CHUNKS
    )
    grad = dot(z, d_pre, ((0,), (0,)))
    half = grad.shape[0] // 2
    odd = (rep_ref[0] & 1) == 1
    low, high = grad[:half], grad[half:]
    bias = jnp.sum(d_pre.astype(F32), axis=0, keepdims=True)
    outer = jnp.sum(hidden * dlogit, axis=0, keepdims=True)
    first = iota((weights_ref.shape[0] // 2 - half, grad.shape[1]), 0)
    aux = jnp.where(first == 0, bias, jnp.where(first == 1, outer, 0.0))
    weights_ref[...] = jnp.concatenate([jnp.where(odd, high, low), aux, jnp.where(odd, low, high), aux], axis=0)
    wait(copies)


def final_kernel(rep_ref, mine_ref, other_ref, keep_ref, *refs):
    away_refs, (sums_ref, grad_ref, bias_ref, outer_ref) = refs[:-4], refs[-4:]
    rows = keep_ref.shape[0] // max(1, len(away_refs))
    for i, away_ref in enumerate(away_refs):
        at = pl.ds(i * rows, rows)
        sums_ref[at, :] = keep_ref[at, :] + away_ref[...].astype(F32)
    if not away_refs:
        sums_ref[...] = keep_ref[...]
    half = grad_ref.shape[0] // 2
    odd = (rep_ref[0] & 1) == 1
    mine, other = mine_ref[...].astype(F32), other_ref[...].astype(F32)
    low = jnp.where(odd, other, mine)
    grad_ref[:half] = low[:half]
    grad_ref[half:] = jnp.where(odd, mine, other)[:half]
    bias_ref[...] = low[half:half + 1]
    outer_ref[...] = low[half + 1:half + 2]


def scatter_kernel(grads_ref, *refs):
    count = len(refs) // 2
    for mask_ref, out_ref in zip(refs[:count], refs[count:]):
        out_ref[...] = dot(mask_ref[...], grads_ref[...]).astype(out_ref.dtype)


def call(kernel, outs, *args, scalar=False, hbm_in=(), hbm_out=(), far_out=(), scratch=()):
    far_out = tuple(far_out) + tuple(hbm_out)
    space = pl.BlockSpec(memory_space=pltpu.VMEM)
    far = pl.BlockSpec(memory_space=pltpu.HBM)
    in_specs = [far if i in hbm_in else space for i in range(len(args))]
    if scalar:
        in_specs[0] = pl.BlockSpec(memory_space=pltpu.SMEM)
    args = [pltpu.with_memory_space_constraint(x, pltpu.HBM) if i in hbm_in else x for i, x in enumerate(args)]
    return pl.pallas_call(
        kernel,
        out_shape=[(pltpu.HBM if i in far_out else pltpu.VMEM)(s, t) for i, (s, t) in enumerate(outs)],
        in_specs=in_specs,
        out_specs=[far if i in hbm_out else space for i in range(len(outs))],
        scratch_shapes=list(scratch),
        compiler_params=pltpu.CompilerParams(vmem_limit_bytes=VMEM_BYTES),
    )(*args)


def swap(x, axis, mask):
    return lax.ppermute(x, axis, [(i, i ^ mask) for i in range(lax.axis_size(axis))])


def rounded(x):
    return lax.reduce_precision(x, exponent_bits=8, mantissa_bits=7)


def reduce_pairs(x, axis, mask):
    mine = rounded(x)
    return mine + swap(mine.astype(BF16), axis, mask).astype(F32)


def reduce_fours(x, axis, mask):
    mine = rounded(x)
    first, second, third = (swap(mine.astype(BF16), axis, mask * k).astype(F32) for k in (1, 2, 3))
    return (mine + first) + (second + third)


def exchange(x, axis):
    return lax.all_to_all(x, axis, split_axis=0, concat_axis=0, tiled=True)


def per_device(
    feats, history, adj_inner, adj_halo, halo_rows, w_self, w_nbr, b_enc,
    edge_owner, edge_rows, labels, w_dec1, b_dec1, w_dec2,
):
    n_dom = lax.axis_size("dom")
    n_rep = lax.axis_size("rep")
    nodes, width = feats.shape
    queries = edge_owner.shape[0]
    cap_halo = halo_rows.shape[1]
    cap = max(2, 4 * queries // n_dom)
    slots = n_dom * cap
    rep = lax.axis_index("rep").astype(I32).reshape(1)

    ends = 2 * queries
    ride = cap_halo % 16 == 0 and cap <= width // 2
    if ride:
        asked = exchange(halo_rows, "dom")
    word, place = call(
        functools.partial(request_kernel, cap, not ride),
        [((n_dom, cap), I32), ((1, ends), I32)],
        edge_owner.T, edge_rows.T, halo_rows,
        far_out=() if ride else (0,),
        hbm_in=(0, 1, 2),
        scratch=(
            pltpu.VMEM((2, queries), I32), pltpu.VMEM((2, queries), I32), pltpu.VMEM(halo_rows.shape, I32),
            pltpu.SemaphoreType.DMA((3,)),
        ),
    )
    if not ride:
        word = exchange(word, "dom")
    agg, base, adj_halo, w_nbr, history = call(
        inner_kernel,
        [
            ((nodes, width), F32), ((nodes, width), F32),
            (adj_halo.shape, BF16), (w_nbr.shape, BF16), (history.shape, BF16),
        ],
        feats, adj_inner, w_self, b_enc.reshape(1, -1), adj_halo, w_nbr, history,
        hbm_in=(0, 1, 2, 3, 4, 5, 6),
        scratch=(
            pltpu.VMEM(feats.shape, BF16), pltpu.VMEM(adj_inner.shape, BF16), pltpu.VMEM(w_self.shape, BF16),
            pltpu.VMEM((1, width), F32), pltpu.SemaphoreType.DMA((7,)),
        ),
    )
    if ride:
        (halo,) = call(
            halo_and_ids_kernel, [((n_dom, cap_halo + SPARE, width), BF16)], asked, word, history
        )
        halo = exchange(halo, "dom")
        ids = jnp.zeros((8, 128), I32)
    else:
        halo, ids = call(
            functools.partial(halo_kernel, cap_halo, cap),
            [((n_dom * cap_halo, width), BF16), ((slots, 1), I32)],
            word, history,
        )
        halo = exchange(halo.reshape(n_dom, cap_halo, width), "dom").reshape(-1, width)
    embed, fetched, got = call(
        functools.partial(embed_kernel, cap if ride else 0),
        [((nodes, width), BF16), ((slots, width), BF16), ((n_dom, cap), I32)],
        agg, base, halo, adj_halo, w_nbr, ids,
        hbm_out=(0, 1),
        scratch=(
            pltpu.VMEM((nodes, width), BF16), pltpu.VMEM((slots, width), BF16),
            pltpu.SemaphoreType.DMA((1,)), pltpu.SemaphoreType.DMA((CHUNKS,)),
        ),
    )
    word = got if ride else word
    fetched = exchange(fetched.reshape(n_dom, cap, width), "dom").reshape(-1, width)
    gather, scatter, target, w1, b1, w2 = call(
        edge_mask_kernel,
        [
            ((ends, slots), BF16), ((slots, ends), BF16), ((queries, 1), F32),
            (w_dec1.shape, BF16), ((1, width), F32), ((1, width), BF16),
        ],
        place, labels.reshape(1, -1), w_dec1, b_dec1.reshape(1, -1), w_dec2.reshape(1, -1),
        hbm_in=(1, 2, 3, 4),
        scratch=(pltpu.VMEM((1, queries), I32), pltpu.SemaphoreType.DMA((4,))),
    )
    half = width // 2
    placed, weights = call(
        decode_kernel,
        [((slots, width), BF16), ((2 * (half + 16), width), F32)],
        rep, fetched, gather, scatter, target, w1, b1, w2,
        scalar=True,
        hbm_out=(0,),
        scratch=(pltpu.VMEM((slots, width), BF16), pltpu.SemaphoreType.DMA((CHUNKS,))),
    )
    back = exchange(placed.reshape(n_dom, cap, width), "dom").reshape(-1, width)
    keep, send = jnp.split(rounded(weights), 2, axis=0)
    weights = keep + swap(send.astype(BF16), "rep", 1).astype(F32)
    if n_rep > 2:
        second, third = swap(keep.astype(BF16), "rep", 2), swap(send.astype(BF16), "rep", 3)
        weights = weights + (second.astype(F32) + third.astype(F32))
    step = 4
    while step < n_rep:
        weights = reduce_pairs(weights, "rep", step)
        step *= 2
    step = 1
    while 4 * step <= n_dom // 2:
        mine = rounded(weights)
        parts = [swap(mine.astype(BF16), "dom", step * k) for k in (1, 2, 3)]
        back, *parts[:2] = lax.optimization_barrier((back, *parts[:2]))
        first, second, third = (part.astype(F32) for part in parts)
        weights = (mine + first) + (second + third)
        step *= 4
    size = nodes // n_rep
    masks = call(
        functools.partial(sum_mask_kernel, cap), [((size, slots), BF16)] * n_rep, rep, word, scalar=True
    )

    block = {}
    for group in (range(n_rep - 1, 0, -2), range(n_rep - 2, -1, -2)):
        outs = call(
            scatter_kernel,
            [((size, width), BF16 if j % 2 else F32) for j in group],
            back, *(masks[j] for j in group),
        )
        block.update(zip(group, outs))
    sums = {j: block[j] + swap(block[j + 1], "rep", 1).astype(F32) for j in reversed(range(0, n_rep, 2))}
    rep_step, away = 2, []
    while rep_step < n_rep:
        for j in range(0, n_rep, 2 * rep_step):
            parts = jnp.split(sums[j + rep_step].astype(BF16), X_PARTS, axis=0)
            away = [swap(part, "rep", rep_step) for part in parts]
            if step < n_dom:
                mine = rounded(weights)
                others = swap(mine.astype(BF16), "dom", step)
                others, away[0] = lax.optimization_barrier((others, away[0]))
                weights = mine + others.astype(F32)
                step *= 2
            if 2 * rep_step < n_rep:
                sums[j] = sums[j] + jnp.concatenate(away, axis=0).astype(F32)
        rep_step *= 2
    while step < n_dom:
        weights = reduce_pairs(weights, "dom", step)
        step *= 2

    weights = rounded(weights).astype(BF16)
    others = swap(weights, "rep", 1)
    grad_embed, grad_dec1, grad_bias1, grad_dec2 = call(
        final_kernel,
        [((size, width), F32), ((width, width), F32), ((1, width), F32), ((1, width), F32)],
        rep, weights, others, sums[0], *away, scalar=True, far_out=(0, 1, 2, 3),
    )
    return embed, grad_embed, grad_dec1, grad_bias1[0], grad_dec2[0]


def solution(mesh):
    placed = (
        P("dom", None), P("dom", None), P("dom", None), P("dom", None), P("dom", None),
        P(), P(), P(),
        P(("dom", "rep"), None), P(("dom", "rep"), None), P(("dom", "rep")),
        P(), P(), P(),
    )
    return jax.shard_map(
        per_device,
        mesh=mesh,
        in_specs=placed,
        out_specs=(P("dom", None), P(("dom", "rep"), None), P(), P(), P()),
        check_vma=False,
    )
```
